256 devices in a mesh: rows: 64 (over z, y, core), rep: 4 (over x).
Axes of the slice: x: 4, y: 4, z: 8, core: 2. Of those that a mesh axis runs over, the one named last changes fastest.
Arguments:
- corpus: bfloat16 [65536, 768], P('rows'), may hold values from -16 to 16
- initial_centroids: float32 [4096, 768], P('rep'), may hold values from -16 to 16
- cand_block: int32 [65536], P('rows'), may hold values from 0 to 63
- leaf_ids: int32 [65536], P('rows'), may hold values from 0 to 4095, as said below
- slot_table: int32 [4096], replicated, may hold values from 0 to 4095, as said below
Outputs:
- coarse_centroids: float32 [4096, 768], P('rep')
- leaf_centroids: float32 [4096, 768], P(('rows', 'rep'))
The draws below stay inside these ranges and needn't reach their ends.
Inputs may be any that keep to these rules, and one draw needn't show every extreme that they name: `leaf_ids`: in each aligned block of 256 rows, for every owner o in 0 .. 63, exactly 4 rows name a leaf l with slot_table[l] // 64 == o. `slot_table`: A permutation of 0 .. 4095.
All inputs are finite; a program needn't handle non-finite values.
Results may differ from the reference program's by a relative error of at most 0.0029.
Values may be sent and summed in bfloat16 or wider, within the bound.
A program may use at most 64 MiB of HBM per device.

```python
import jax
import jax.numpy as jnp
from jax import lax

D = 768
K = 4096
BLOCK = 64
ITERS = 2
VEC_DEV = 1024
LEAF_DEV = 64
VECTORS = 65536
LEAVES = 4096
SENDS = 256
N_ROWS = 64


def block_draw(key):
    key = jax.random.fold_in(key, 11)
    return jax.random.randint(key, (VECTORS,), 0, K // BLOCK, dtype=jnp.int32)


def centre_draw(key):
    scale_key = jax.random.fold_in(key, 13)
    value_key = jax.random.fold_in(key, 14)
    scales = jnp.exp(jax.random.uniform(scale_key, (K, 1), jnp.float32, jnp.log(0.2), jnp.log(1.5)))
    return jax.random.normal(value_key, (K, D), jnp.float32) * scales


def slot_draw(key):
    return jax.random.permutation(jax.random.fold_in(key, 21), LEAVES).astype(jnp.int32)


def draw_corpus(key, part):
    chosen = block_draw(key)
    member = jax.random.randint(jax.random.fold_in(key, 12), (VECTORS,), 0, BLOCK, dtype=jnp.int32)
    centres = centre_draw(key)
    key = jax.random.fold_in(key, 1)
    noise = 0.7 * jax.random.normal(key, (VECTORS, D), jnp.float32)
    return (centres[chosen * BLOCK + member] + noise).astype(jnp.bfloat16)


def draw_initial_centroids(key, part):
    centres = centre_draw(key)
    key = jax.random.fold_in(key, 2)
    return centres + 0.3 * jax.random.normal(key, (K, D), jnp.float32)


def draw_cand_block(key, part):
    return block_draw(key)


def draw_slot_table(key, part):
    return slot_draw(key)


def draw_leaf_ids(key, part):
    table = slot_draw(key)
    key = jax.random.fold_in(key, 4)
    groups = VECTORS // SENDS
    order_keys = jax.random.split(jax.random.fold_in(key, 1), groups)
    orders = jax.vmap(lambda sub: jax.random.permutation(sub, SENDS))(order_keys).astype(jnp.int32)
    owners = orders % N_ROWS
    locals_drawn = jax.random.randint(jax.random.fold_in(key, 2), (groups, SENDS), 0, LEAF_DEV, dtype=jnp.int32)
    positions = owners * LEAF_DEV + locals_drawn
    inverse = jnp.zeros((LEAVES,), jnp.int32).at[table].set(jnp.arange(LEAVES, dtype=jnp.int32))
    return inverse[positions].reshape(VECTORS)


def setup_inputs(seed: int = 0) -> dict:
    splits = jax.random.split(jax.random.key(seed), 6)
    return {
        "corpus": draw_corpus(jax.random.fold_in(splits[5], 71), 0),
        "initial_centroids": draw_initial_centroids(jax.random.fold_in(splits[5], 71), 0),
        "cand_block": draw_cand_block(jax.random.fold_in(splits[5], 71), 0),
        "leaf_ids": draw_leaf_ids(jax.random.fold_in(splits[5], 71), 0),
        "slot_table": draw_slot_table(jax.random.fold_in(splits[5], 71), 0),
    }


def weigh(row_tile, chosen, table_half, centre_norms):
    offsets = jnp.arange(BLOCK, dtype=jnp.int32)
    columns = chosen[:, None] * BLOCK + offsets[None, :]
    picked = table_half[columns].astype(jnp.float32)
    entries = row_tile.astype(jnp.float32)
    products = jnp.einsum("bd,bmd->bm", entries, picked)
    distance = jnp.sum(entries * entries, axis=1)[:, None] + centre_norms[columns] - 2.0 * products
    kernel = 1.0 / (1.0 + distance / D)
    weights = (kernel / jnp.sum(kernel, axis=1, keepdims=True)).astype(jnp.bfloat16)
    return columns, entries, weights


def reference(corpus, initial_centroids, cand_block, leaf_ids, slot_table):
    groups = VECTORS // VEC_DEV
    row_blocks = corpus.reshape(groups, VEC_DEV, D)
    block_ids = cand_block.reshape(groups, VEC_DEV)
    centroids = initial_centroids
    previous = centroids
    for iteration in range(ITERS):
        table_half = centroids.astype(jnp.bfloat16)
        centre_norms = jnp.sum(centroids * centroids, axis=1)

        def accumulate(running, inputs):
            row_tile, chosen = inputs
            columns, entries, weights = weigh(row_tile, chosen, table_half, centre_norms)
            wide_weights = weights.astype(jnp.float32)
            flat_ids = columns.reshape(-1)
            contrib = (wide_weights[:, :, None] * entries[:, None, :]).reshape(-1, D)
            totals = running[0] + jax.ops.segment_sum(contrib, flat_ids, num_segments=K)
            counts = running[1] + jax.ops.segment_sum(wide_weights.reshape(-1), flat_ids, num_segments=K)
            return (totals, counts), None

        start = (jnp.zeros((K, D), jnp.float32), jnp.zeros((K,), jnp.float32))
        (totals, counts), _ = lax.scan(accumulate, start, (row_blocks, block_ids))
        previous = centroids
        centroids = 0.5 * centroids + 0.5 * totals / (counts + 1.0)[:, None]
    prev_half = previous.astype(jnp.bfloat16)
    prev_norms = jnp.sum(previous * previous, axis=1)
    final_half = centroids.astype(jnp.bfloat16)

    def rebuild(running, inputs):
        row_tile, chosen = inputs
        columns, entries, weights = weigh(row_tile, chosen, prev_half, prev_norms)
        rebuilt = jnp.einsum("bm,bmd->bd", weights.astype(jnp.float32), final_half[columns].astype(jnp.float32))
        return running, (entries - rebuilt).astype(jnp.bfloat16)

    _, residual = lax.scan(rebuild, jnp.zeros((), jnp.float32), (row_blocks, block_ids))
    residual = residual.reshape(VECTORS, D)
    slot_ids = slot_table[leaf_ids]
    leaf_sums = jax.ops.segment_sum(residual.astype(jnp.float32), slot_ids, num_segments=LEAVES)
    leaf_counts = jax.ops.segment_sum(jnp.ones((VECTORS,), jnp.float32), slot_ids, num_segments=LEAVES)
    return centroids, leaf_sums / (leaf_counts + 1.0)[:, None]
```

```python
import functools

import jax
import jax.numpy as jnp
from jax import lax
from jax.experimental import pallas as pl
from jax.experimental.pallas import tpu as pltpu
from jax.sharding import PartitionSpec as P

D = 768
BLOCK = 64
LANES = 128
WIDE = D + LANES
NZ, NY, NC, NX = 8, 4, 2, 4
OWNERS = NZ * NY * NC
OWN = 16
ROWS = 1024
CENTS = 1024
SENDS = 256
TILE = 256
STEPS = CENTS // TILE
LEAF_DEV = 64
SPLIT = 640
F32, BF16 = jnp.float32, jnp.bfloat16
MESH = pl.DeviceIdType.MESH
ANYWHERE = pl.BlockSpec(memory_space=pltpu.VMEM)
LIMIT = 48 * 1024 * 1024


def iota(shape, axis):
    return lax.broadcasted_iota(jnp.int32, shape, axis)


def dot(a, b, ca=1, cb=0):
    return lax.dot_general(a, b, (((ca,), (cb,)), ((), ())), preferred_element_type=F32)


def place():
    r = lax.axis_index("rows")
    return r // (NY * NC), lax.rem(r // NC, NY), lax.rem(r, NC), lax.axis_index("rep")


def row_index(z, y, c):
    return (z * NY + y) * NC + c


def row_norms(corpus):
    square = jnp.square(corpus.astype(F32))
    high = square.astype(BF16)
    low = (square - high.astype(F32)).astype(BF16)
    ones = jnp.ones((8, D), BF16)
    return (dot(ones, high, 1, 1) + dot(ones, low, 1, 1))[:1]


def tile_weights(cents, corpus, norms, cand, first_block):
    centre = jnp.sum(cents * cents, axis=1, keepdims=True)
    products = dot(cents.astype(BF16), corpus, 1, 1)
    kernel = 1.0 / (1.0 + (norms + centre - 2.0 * products) / D)
    parts, compact = [], None
    for b in range(TILE // BLOCK):
        piece = kernel[b * BLOCK : (b + 1) * BLOCK]
        total = jnp.sum(piece, axis=0, keepdims=True)
        piece = jnp.where(cand == first_block + b, piece / total, 0.0).astype(BF16)
        parts.append(piece)
        wide = piece.astype(F32)
        compact = wide if compact is None else compact + wide
    return jnp.concatenate(parts, axis=0), compact


def encode_counts(total):
    high = total.astype(BF16).astype(F32)
    return jnp.where(iota(total.shape, total.ndim - 1) < LANES // 2, high, total - high).astype(BF16)


def store_part(part_ref, weights, corpus):
    part_ref[:, :D] = dot(weights, corpus).astype(BF16)
    counts = jnp.sum(weights.astype(F32), axis=1, keepdims=True)
    part_ref[:, D:] = encode_counts(jnp.broadcast_to(counts, (weights.shape[0], LANES)))


def first_kernel(corpus_ref, c0_ref, cand_ref, part_ref, norm_ref):
    step = pl.program_id(0)

    @pl.when(step == 0)
    def _():
        norm_ref[...] = row_norms(corpus_ref[...])

    corpus = corpus_ref[...]
    weights, _ = tile_weights(c0_ref[...], corpus, norm_ref[...], cand_ref[...], step * (TILE // BLOCK))
    store_part(part_ref, weights, corpus)


def positions(leaf, slots):
    side = slots.shape[0]
    upper = (iota((side, ROWS), 0) == (leaf >> 6)).astype(BF16)
    lower = iota((side, ROWS), 0) == (leaf & 63)

    def look(values):
        found = dot(values.astype(F32).astype(BF16), upper, 0, 0)
        return jnp.sum(jnp.where(lower, found, 0.0), axis=0, keepdims=True)

    owner, slot = look(slots >> 6).astype(jnp.int32), look(slots & 63)
    hits = iota((OWNERS, ROWS), 0) == owner
    before = (iota((SENDS, SENDS), 0) < iota((SENDS, SENDS), 1)).astype(BF16)
    ranks = []
    for q in range(ROWS // SENDS):
        own = hits[:, q * SENDS : (q + 1) * SENDS]
        ahead = dot(jnp.where(own, 1.0, 0.0).astype(BF16), before)
        ranks.append(jnp.sum(jnp.where(own, ahead, 0.0), axis=0, keepdims=True))
    return owner, slot, jnp.concatenate(ranks, axis=1).astype(jnp.int32)


def second_kernel(corpus_ref, c0_ref, d_ref, cand_ref, leaf_ref, slots_ref, part_ref, wsend_ref, csend_ref, norm_ref, comp_ref):
    step = pl.program_id(0)

    @pl.when(step == 0)
    def _():
        norm_ref[...] = row_norms(corpus_ref[...])
        comp_ref[...] = jnp.zeros_like(comp_ref)

    corpus = corpus_ref[...]
    cents = 0.5 * c0_ref[...] + d_ref[...].astype(F32)
    weights, compact = tile_weights(cents, corpus, norm_ref[...], cand_ref[...], step * (TILE // BLOCK))
    store_part(part_ref, weights, corpus)
    comp_ref[...] += compact

    @pl.when(step == STEPS - 1)
    def _():
        owner, slot, rank = positions(leaf_ref[...], slots_ref[...])
        z, y, c = owner >> 3, (owner >> 1) & 3, owner & 1
        spot = (c * NY + y) * NZ + z
        quarter = iota((1, ROWS), 1) >> 8
        target = spot * 16 + quarter * 4 + rank
        block = cand_ref[...].astype(F32)
        fill = iota((BLOCK, ROWS), 0)
        meta = jnp.where(fill == 0, slot, jnp.where(fill == 1, block, 0.0))
        load = jnp.concatenate([comp_ref[...], meta], axis=0).astype(BF16)
        for t in range(ROWS // TILE):
            pick = (iota((TILE, ROWS), 0) + t * TILE == target).astype(BF16)
            wsend_ref[pl.ds(t * TILE, TILE), :] = dot(pick, load, 1, 1).astype(BF16)
        x = lax.axis_index("rep")
        mine = pl.ds(pl.multiple_of(x * SENDS, SENDS), SENDS)
        short = jnp.where(quarter == x, spot * 4 + rank, -1)
        whole = (iota((SENDS, ROWS), 0) == short).astype(BF16)
        pick = whole[:, :SENDS] + whole[:, SENDS : 2 * SENDS] + whole[:, 2 * SENDS : 3 * SENDS] + whole[:, 3 * SENDS :]
        csend_ref[:, :D] = dot(pick, corpus_ref[mine, :]).astype(BF16)
        csend_ref[:, D:] = dot(whole, load, 1, 1).astype(BF16)


class Link:
    def __init__(self, send, recv):
        self.send, self.recv, self.used, self.sent = send, recv, 0, []

    def slots(self, count):
        first = self.used
        self.used += count
        return first

    def make(self, src, dst, slot, device):
        return pltpu.make_async_remote_copy(
            src_ref=src, dst_ref=dst, send_sem=self.send.at[slot], recv_sem=self.recv.at[slot],
            device_id=device, device_id_type=MESH,
        )

    def start(self, src, dst, slot, device):
        copy = self.make(src, dst, slot, device)
        copy.start()
        self.sent.append(copy)

    def arrived(self, dst, slot, device):
        self.make(dst, dst, slot, device).wait_recv()

    def finish(self):
        for copy in self.sent:
            copy.wait_send()


class Axis:
    def __init__(self, size, me, peer):
        self.size, self.me, self.peer = size, me, peer

    def at(self, k):
        return lax.rem(self.me + k, self.size)

    def back(self, k):
        return lax.rem(self.me + self.size - k, self.size)


class Group:
    def __init__(self, link, first, second, lead, columns, gathered, scratch):
        self.link, self.first, self.second, self.lead = link, first, second, lead
        self.columns = pl.ds(columns[0], columns[1] - columns[0])
        self.gathered = pl.ds(gathered[0], gathered[1] - gathered[0])
        self.counted = columns[1] == WIDE
        self.land2, self.own2, self.land3 = scratch
        self.s_core, self.s_first, self.s_second = link.slots(first.size), link.slots(first.size), link.slots(second.size)
        self.g_first, self.g_second, self.g_core = link.slots(first.size), link.slots(second.size), link.slots(first.size)

    def block(self, ref, i, columns):
        return ref.at[i, :, :, columns] if self.lead else ref.at[:, i, :, columns]

    def round(self, total):
        if not self.counted:
            return total.astype(BF16)
        body, tail = total[..., :-LANES], total[..., -LANES:]
        shape = tail.shape
        tail = tail.reshape(-1, LANES)
        tail = tail + pltpu.roll(tail, LANES // 2, 1)
        return jnp.concatenate([body.astype(BF16), encode_counts(tail).reshape(shape)], axis=-1)

    def to_core(self, part, c, land1, other):
        for k in range(1, self.first.size + 1):
            i = self.first.at(k)
            self.link.start(
                self.block(part.at[1 - c], i, self.columns), self.block(land1, i, self.columns), self.s_core + k - 1, other
            )

    def to_first(self, part, c, land1, stage, other):
        for k in range(1, self.first.size + 1):
            i = self.first.at(k)
            here = self.block(land1, i, self.columns)
            self.link.arrived(here, self.s_core + k - 1, other)
            total = self.block(part.at[c], i, self.columns)[...].astype(F32) + here[...].astype(F32)
            if k == self.first.size:
                self.own2[...] = total
            else:
                out = self.block(stage, i, self.columns)
                out[...] = self.round(total)
                self.link.start(out, self.land2.at[k - 1], self.s_first + k - 1, self.first.peer(i))

    def to_second(self, stage):
        for k in range(1, self.first.size):
            self.link.arrived(self.land2.at[k - 1], self.s_first + k - 1, self.first.peer(self.first.back(k)))
        for k in range(1, self.second.size + 1):
            j = self.second.at(k)
            total = self.own2[j]
            for s in range(self.first.size - 1):
                total = total + self.land2[s, j].astype(F32)
            if k == self.second.size:
                self.own3 = total
            else:
                out = stage.at[j, :, self.columns]
                out[...] = self.round(total)
                self.link.start(out, self.land3.at[k - 1], self.s_second + k - 1, self.second.peer(j))

    def total(self):
        total = self.own3
        for k in range(1, self.second.size):
            self.link.arrived(self.land3.at[k - 1], self.s_second + k - 1, self.second.peer(self.second.back(k)))
            total = total + self.land3[k - 1].astype(F32)
        return total

    def spot(self, half, i, j):
        return half.at[i, j, :, self.gathered] if self.lead else half.at[j, i, :, self.gathered]

    def gather_second(self, half):
        mine = self.spot(half, self.first.me, self.second.me)
        for k in range(1, self.second.size):
            self.link.start(mine, mine, self.g_second + k, self.second.peer(self.second.at(k)))

    def gather_first(self, half, other):
        for k in range(1, self.second.size):
            j = self.second.back(k)
            self.link.arrived(self.spot(half, self.first.me, j), self.g_second + k, self.second.peer(j))
        mine = self.block(half, self.first.me, self.gathered)
        for k in range(1, self.first.size):
            self.link.start(mine, mine, self.g_first + k, self.first.peer(self.first.at(k)))
        self.link.start(mine, mine, self.g_core, other)

    def gather_core(self, half, other):
        for k in range(1, self.first.size):
            i = self.first.back(k)
            here = self.block(half, i, self.gathered)
            self.link.arrived(here, self.g_first + k, self.first.peer(i))
            self.link.start(here, here, self.g_core + k, other)

    def gathered_core(self, half, other):
        for k in range(self.first.size):
            self.link.arrived(self.block(half, self.first.back(k), self.gathered), self.g_core + k, other)


def greet(peers):
    barrier = pltpu.get_barrier_semaphore()
    for peer in peers:
        pl.semaphore_signal(barrier, inc=1, device_id=peer, device_id_type=MESH)
    pl.semaphore_wait(barrier, len(peers))


class Route:
    def __init__(self, link, src, near, middle, got, mix=None):
        self.link, self.src, self.near, self.middle, self.got, self.mix = link, src, near, middle, got, mix
        self.s_core, self.s_y, self.s_z = link.slots(1), link.slots(2 * NY), link.slots(NZ)

    def to_core(self, c, other):
        self.link.start(self.src.at[1 - c], self.near, self.s_core, other)

    def to_y(self, c, ys, other):
        self.link.arrived(self.near, self.s_core, other)
        for s, ref in enumerate((self.src.at[c], self.near)):
            for k in range(1, NY):
                i = ys.at(k)
                self.link.start(ref.at[i], self.middle.at[ys.me, s], self.s_y + 2 * k + s, ys.peer(i))
            self.middle[ys.me, s] = ref[ys.me]

    def to_z(self, ys, zs):
        for k in range(1, NY):
            i = ys.back(k)
            for s in range(2):
                self.link.arrived(self.middle.at[i, s], self.s_y + 2 * k + s, ys.peer(i))
        if self.mix is None:
            blocks = lambda j: self.middle.at[:, :, j]
        else:
            d, s = iota((SENDS, SENDS), 0), iota((SENDS, SENDS), 1)
            order = (s == ((d & 31) >> 2) * 32 + (d >> 5) * 4 + (d & 3)).astype(BF16)
            mixed = dot(order, self.middle[...].reshape(SENDS, WIDE)).astype(BF16)
            self.mix[...] = mixed.reshape(self.mix.shape)
            blocks = lambda j: self.mix.at[j]
        for k in range(1, NZ):
            j = zs.at(k)
            self.link.start(blocks(j), self.got.at[zs.me], self.s_z + k, zs.peer(j))
        self.got[zs.me] = blocks(zs.me)[...]

    def finish(self, zs):
        for k in range(1, NZ):
            j = zs.back(k)
            self.link.arrived(self.got.at[j], self.s_z + k, zs.peer(j))


def reduce_kernel(routed, *refs):
    refs = list(refs)
    take = lambda n: [refs.pop(0) for _ in range(n)]
    part, d_old = take(2)
    sends = take(2 * routed)
    table, d_own = take(2)
    gots = take(2 * routed)
    land1, stage1, stage2, a2, a2o, a3, b2, b2o, b3, send, recv = take(11)
    z, y, c, x = place()
    other = (row_index(z, y, 1 - c), x)
    zs = Axis(NZ, z, lambda i: (row_index(i, y, c), x))
    ys = Axis(NY, y, lambda i: (row_index(z, i, c), x))
    link = Link(send, recv)
    groups = (
        Group(link, ys, zs, True, (0, SPLIT), (0, SPLIT), (a2, a2o, a3)),
        Group(link, zs, ys, False, (SPLIT, WIDE), (SPLIT, D), (b2, b2o, b3)),
    )
    routes = []
    if routed:
        wl1, wl2, cl1, cl2, cmix = take(5)
        routes = [Route(link, sends[0], wl1, wl2, gots[0]), Route(link, sends[1], cl1, cl2, gots[1], cmix)]
    greet([other] + [zs.peer(zs.at(k)) for k in range(1, NZ)] + [ys.peer(ys.at(k)) for k in range(1, NY)])
    for g in groups:
        g.to_core(part, c, land1, other)
    for r in routes:
        r.to_core(c, other)
    for g in groups:
        g.to_first(part, c, land1, stage1, other)
    for r in routes:
        r.to_y(c, ys, other)
    for g in groups:
        g.to_second(stage2)
    for r in routes:
        r.to_z(ys, zs)
    totals = [g.total() for g in groups]
    counts = totals[1][..., -LANES:]
    counts = (counts + pltpu.roll(counts, LANES // 2, 1))[:, :1]
    sums = jnp.concatenate([totals[0], totals[1][..., :-LANES]], axis=-1)
    fresh = 0.5 * d_old[...] + 0.5 * (sums / (counts + 1.0))
    d_own[...] = fresh
    table[c, y, z] = fresh.astype(BF16)
    half = table.at[c]
    for g in groups:
        g.gather_second(half)
    for g in groups:
        g.gather_first(half, other)
    for g in groups:
        g.gather_core(half, other)
    for g in groups:
        g.gathered_core(table.at[1 - c], other)
    for r in routes:
        r.finish(zs)
    link.finish()


def all_reduce(part, d_old, wsend=None, csend=None):
    routed = wsend is not None
    args = [part.reshape(NC, NY, NZ, OWN, WIDE), d_old]
    outs = [jax.ShapeDtypeStruct((NC, NY, NZ, OWN, D), BF16), jax.ShapeDtypeStruct((OWN, D), F32)]
    wide_b = WIDE - SPLIT
    scratch = [
        pltpu.VMEM((NY, NZ, OWN, WIDE), BF16),
        pltpu.VMEM((NY, NZ, OWN, WIDE), BF16),
        pltpu.VMEM((NZ, OWN, WIDE), BF16),
        pltpu.VMEM((NY - 1, NZ, OWN, SPLIT), BF16),
        pltpu.VMEM((NZ, OWN, SPLIT), F32),
        pltpu.VMEM((NZ - 1, OWN, SPLIT), BF16),
        pltpu.VMEM((NZ - 1, NY, OWN, wide_b), BF16),
        pltpu.VMEM((NY, OWN, wide_b), F32),
        pltpu.VMEM((NY - 1, OWN, wide_b), BF16),
        pltpu.SemaphoreType.DMA((112,)),
        pltpu.SemaphoreType.DMA((112,)),
    ]
    if routed:
        args += [wsend.reshape(NC, NY, NZ, 16, LANES), csend.reshape(NC, NY, 32, WIDE)]
        outs += [
            jax.ShapeDtypeStruct((NZ, NY, NC, 16, LANES), BF16),
            jax.ShapeDtypeStruct((NZ, 32, WIDE), BF16),
        ]
        scratch += [
            pltpu.VMEM((NY, NZ, 16, LANES), BF16),
            pltpu.VMEM((NY, NC, NZ, 16, LANES), BF16),
            pltpu.VMEM((NY, 32, WIDE), BF16),
            pltpu.VMEM((NY, NC, 32, WIDE), BF16),
            pltpu.VMEM((NZ, 32, WIDE), BF16),
        ]
    return pl.pallas_call(
        functools.partial(reduce_kernel, routed),
        out_shape=outs,
        in_specs=[ANYWHERE] * len(args),
        out_specs=[ANYWHERE] * len(outs),
        scratch_shapes=scratch,
        compiler_params=pltpu.CompilerParams(
            collective_id=1 + routed, has_side_effects=True, vmem_limit_bytes=LIMIT
        ),
        name="route" if routed else "reduce",
    )(*args)


def leaf_kernel(c0_ref, d_ref, wgot_ref, cgot_ref, c2_ref, leaf_ref, count_ref, pairs_ref):
    step = pl.program_id(0)

    @pl.when(step == 0)
    def _():
        eye = (iota((LANES, LANES), 0) == iota((LANES, LANES), 1)).astype(BF16)
        turned = dot(eye, wgot_ref[...], 1, 1)
        weights, slot, block = turned[:BLOCK], turned[BLOCK : BLOCK + 1], turned[BLOCK + 1 : BLOCK + 2]
        places = iota((LEAF_DEV, ROWS), 0)
        chosen = jnp.where(places == slot.astype(jnp.int32), 1.0, 0.0)
        count_ref[...] = jnp.broadcast_to(jnp.sum(chosen, axis=1, keepdims=True), (LEAF_DEV, LANES))
        chosen = chosen.astype(BF16)
        for b in range(0, CENTS // BLOCK, 2):
            both = jnp.concatenate([jnp.where(block == b + s, weights, 0.0) for s in range(2)], axis=0)
            pairs_ref[b // 2] = dot(chosen, both.astype(BF16), 1, 1)
        corpus = cgot_ref[...]
        turned = dot(eye, corpus[:, D:], 1, 1)
        slot = turned[BLOCK : BLOCK + 1].astype(jnp.int32)
        chosen = (iota((LEAF_DEV, SENDS), 0) == slot).astype(BF16)
        leaf_ref[...] = dot(chosen, corpus[:, :D])

    cents = 0.25 * c0_ref[...] + d_ref[...].astype(F32)
    c2_ref[...] = cents
    half = cents.astype(BF16)
    pairs = TILE // LANES
    mixed = jnp.concatenate([pairs_ref[step * pairs + s] for s in range(pairs)], axis=1)
    high = mixed.astype(BF16)
    low = (mixed - high.astype(F32)).astype(BF16)
    leaf_ref[...] -= dot(high, half) + dot(low, half)


def share_kernel(leaf, count, out, land, send, recv):
    z, y, c, x = place()
    row = row_index(z, y, c)
    xs = Axis(NX, x, lambda i: (row, i))
    link = Link(send, recv)
    greet([xs.peer(xs.at(k)) for k in range(1, NX)])
    for k in range(1, NX):
        i = xs.at(k)
        link.start(leaf.at[i], land.at[k - 1], k - 1, xs.peer(i))
    total = leaf[x]
    for k in range(1, NX):
        link.arrived(land.at[k - 1], k - 1, xs.peer(xs.back(k)))
        total = total + land[k - 1]
    out[...] = total / (count[x][:, :1] + 1.0)
    link.finish()


def on_device(corpus, initial_centroids, cand_block, leaf_ids, slot_table):
    x = lax.axis_index("rep")
    cand = (cand_block - x * (CENTS // BLOCK)).reshape(1, ROWS)
    leaf = leaf_ids.reshape(1, ROWS)
    slots = slot_table.reshape(64, 64)
    fixed = lambda *shape: pl.BlockSpec(shape, lambda t: (0,) * len(shape))
    tiled = lambda width: pl.BlockSpec((TILE, width), lambda t: (t, 0))
    params = pltpu.CompilerParams(vmem_limit_bytes=LIMIT)
    part = pl.pallas_call(
        first_kernel,
        grid=(STEPS,),
        out_shape=jax.ShapeDtypeStruct((CENTS, WIDE), BF16),
        in_specs=[fixed(ROWS, D), tiled(D), fixed(1, ROWS)],
        out_specs=tiled(WIDE),
        scratch_shapes=[pltpu.VMEM((1, ROWS), F32)],
        compiler_params=params,
        name="first",
    )(corpus, initial_centroids, cand)
    d1, d1_own = all_reduce(part, jnp.zeros((OWN, D), F32))
    part, wsend, csend = pl.pallas_call(
        second_kernel,
        grid=(STEPS,),
        out_shape=[
            jax.ShapeDtypeStruct((CENTS, WIDE), BF16),
            jax.ShapeDtypeStruct((ROWS, LANES), BF16),
            jax.ShapeDtypeStruct((SENDS, WIDE), BF16),
        ],
        in_specs=[fixed(ROWS, D), tiled(D), tiled(D), fixed(1, ROWS), fixed(1, ROWS), fixed(64, 64)],
        out_specs=[tiled(WIDE), fixed(ROWS, LANES), fixed(SENDS, WIDE)],
        scratch_shapes=[pltpu.VMEM((1, ROWS), F32), pltpu.VMEM((BLOCK, ROWS), F32)],
        compiler_params=params,
        name="second",
    )(corpus, initial_centroids, d1.reshape(CENTS, D), cand, leaf, slots)
    d2, _, wgot, cgot = all_reduce(part, d1_own, wsend, csend)
    c2, partial, count = pl.pallas_call(
        leaf_kernel,
        grid=(STEPS,),
        out_shape=[
            jax.ShapeDtypeStruct((CENTS, D), F32),
            jax.ShapeDtypeStruct((LEAF_DEV, D), F32),
            jax.ShapeDtypeStruct((LEAF_DEV, LANES), F32),
        ],
        in_specs=[tiled(D), tiled(D), fixed(ROWS, LANES), fixed(SENDS, WIDE)],
        out_specs=[tiled(D), fixed(LEAF_DEV, D), fixed(LEAF_DEV, LANES)],
        scratch_shapes=[pltpu.VMEM((CENTS // LANES, LEAF_DEV, LANES), F32)],
        compiler_params=params,
        name="leaves",
    )(initial_centroids, d2.reshape(CENTS, D), wgot.reshape(ROWS, LANES), cgot.reshape(SENDS, WIDE))
    per = LEAF_DEV // NX
    leaves = pl.pallas_call(
        share_kernel,
        out_shape=jax.ShapeDtypeStruct((per, D), F32),
        in_specs=[ANYWHERE] * 2,
        out_specs=ANYWHERE,
        scratch_shapes=[
            pltpu.VMEM((NX - 1, per, D), F32),
            pltpu.SemaphoreType.DMA((NX - 1,)),
            pltpu.SemaphoreType.DMA((NX - 1,)),
        ],
        compiler_params=pltpu.CompilerParams(collective_id=3, has_side_effects=True),
        name="share",
    )(partial.reshape(NX, per, D), count.reshape(NX, per, LANES))
    return c2, leaves


def solution(mesh):
    in_specs = (P("rows", None), P("rep", None), P("rows"), P("rows"), P())
    out_specs = (P("rep", None), P(("rows", "rep"), None))
    return jax.shard_map(
        on_device, mesh=mesh, in_specs=in_specs, out_specs=out_specs, check_vma=False
    )
```

```python
import functools

import jax
import jax.numpy as jnp
from jax import lax
from jax.experimental import pallas as pl
from jax.experimental.pallas import tpu as pltpu
from jax.sharding import PartitionSpec as P

D = 768
BLOCK = 64
LANES = 128
WIDE = D + LANES
NZ, NY, NC, NX = 8, 4, 2, 4
OWNERS = NZ * NY * NC
ROWS = 1024
CENTS = 1024
SENDS = 256
TILE = 256
LEAF_DEV = 64
CHUNKS, TILES = 2, 4
HALF = D // 2
LEFT = LANES + HALF
F32, BF16 = jnp.float32, jnp.bfloat16
MESH = pl.DeviceIdType.MESH
ANYWHERE = pl.BlockSpec(memory_space=pltpu.VMEM)
LIMIT = 56 * 1024 * 1024
SEMAPHORES = 4 * (4 + 8 + 8 + 8 + 16 + 4) + 2 * (1 + 8 + 8) + 4


def iota(shape, axis):
    return lax.broadcasted_iota(jnp.int32, shape, axis)


def dot(a, b, ca=1, cb=0):
    return lax.dot_general(a, b, (((ca,), (cb,)), ((), ())), preferred_element_type=F32)


def place():
    r = lax.axis_index("rows")
    return r // (NY * NC), lax.rem(r // NC, NY), lax.rem(r, NC), lax.axis_index("rep")


def row_index(z, y, c):
    return (z * NY + y) * NC + c


def row_norms(corpus):
    square = jnp.square(corpus.astype(F32))
    high = square.astype(BF16)
    low = (square - high.astype(F32)).astype(BF16)
    ones = jnp.ones((8, D), BF16)
    return (dot(ones, high, 1, 1) + dot(ones, low, 1, 1))[:1]


def tile_weights(cents, corpus, norms, cand, first_block):
    centre = jnp.sum(cents * cents, axis=1, keepdims=True)
    products = dot(cents.astype(BF16), corpus, 1, 1)
    kernel = 1.0 / (1.0 + (norms + centre - 2.0 * products) / D)
    parts, compact = [], None
    for b in range(TILE // BLOCK):
        piece = kernel[b * BLOCK : (b + 1) * BLOCK]
        total = jnp.sum(piece, axis=0, keepdims=True)
        piece = jnp.where(cand == first_block + b, piece / total, 0.0).astype(BF16)
        parts.append(piece)
        wide = piece.astype(F32)
        compact = wide if compact is None else compact + wide
    return jnp.concatenate(parts, axis=0), compact


def encode_counts(total):
    high = total.astype(BF16).astype(F32)
    return jnp.where(iota(total.shape, total.ndim - 1) < LANES // 2, high, total - high)


def both_parts(counts):
    shape = counts.shape
    counts = counts.reshape(-1, LANES)
    return (counts + pltpu.roll(counts, LANES // 2, 1)).reshape(shape)


def rounded(total):
    counts = encode_counts(both_parts(total[..., :LANES]))
    return jnp.concatenate([counts.astype(BF16), total[..., LANES:].astype(BF16)], axis=-1)


def in_lanes(ref):
    values = ref[...]
    return jnp.concatenate([values[i : i + 1] for i in range(values.shape[0])], axis=1)


def positions(leaf, slots):
    upper = (iota((slots.shape[0], ROWS), 0) == (leaf >> 7)).astype(BF16)
    lower = iota((slots.shape[1], ROWS), 0) == (leaf & 127)

    def look(values):
        found = dot(values.astype(F32).astype(BF16), upper, 0, 0)
        return jnp.sum(jnp.where(lower, found, 0.0), axis=0, keepdims=True)

    owner, slot = look(slots >> 6).astype(jnp.int32), look(slots & 63)
    hits = iota((OWNERS, ROWS), 0) == owner
    before = (iota((SENDS, SENDS), 0) < iota((SENDS, SENDS), 1)).astype(BF16)
    ranks = []
    for q in range(ROWS // SENDS):
        own = hits[:, q * SENDS : (q + 1) * SENDS]
        ahead = dot(jnp.where(own, 1.0, 0.0).astype(BF16), before)
        ranks.append(jnp.sum(jnp.where(own, ahead, 0.0), axis=0, keepdims=True))
    return owner, slot, jnp.concatenate(ranks, axis=1).astype(jnp.int32)


class Link:
    def __init__(self, send, recv):
        self.send, self.recv, self.used, self.sent = send, recv, 0, []

    def slots(self, count):
        first = self.used
        self.used += count
        return first

    def make(self, src, dst, out, into, device):
        return pltpu.make_async_remote_copy(
            src_ref=src, dst_ref=dst, send_sem=self.send.at[out], recv_sem=self.recv.at[into],
            device_id=device, device_id_type=MESH,
        )

    def start(self, src, dst, out, into, device, when=None):
        copy = self.make(src, dst, out, into, device)
        if when is None:
            copy.start()
        else:
            pl.when(when)(copy.start)
        self.sent.append((copy, when))

    def arrived(self, dst, into, device):
        self.make(dst, dst, into, into, device).wait_recv()

    def finish(self):
        for copy, when in self.sent:
            if when is None:
                copy.wait_send()
            else:
                pl.when(when)(copy.wait_send)


class Axis:
    def __init__(self, size, me, peer):
        self.size, self.me, self.peer = size, me, peer

    def at(self, k):
        return lax.rem(self.me + k, self.size)

    def back(self, k):
        return lax.rem(self.me + self.size - k, self.size)


class Here:
    def __init__(self):
        z, y, c, x = place()
        self.z, self.y, self.c, self.x = z, y, c, x
        row = row_index(z, y, c)
        self.zs = Axis(NZ, z, lambda i: (row_index(i, y, c), x))
        self.ys = Axis(NY, y, lambda i: (row_index(z, i, c), x))
        self.xs = Axis(NX, x, lambda i: (row, i))
        self.other = (row_index(z, y, 1 - c), x)

    def greet(self):
        barrier = pltpu.get_barrier_semaphore()
        peers = [self.other] + [a.peer(a.at(k)) for a in (self.zs, self.ys, self.xs) for k in range(1, a.size)]
        for peer in peers:
            pl.semaphore_signal(barrier, inc=1, device_id=peer, device_id_type=MESH)
        return lambda: pl.semaphore_wait(barrier, len(peers))


class Chunk:
    def __init__(self, here, link, part, own1, land1, stage1, land2, own2, stage2, land3, own3, change, table):
        self.here, self.link = here, link
        self.part, self.own1, self.land1, self.stage1, self.land2, self.own2 = part, own1, land1, stage1, land2, own2
        self.stage2, self.land3, self.own3, self.change, self.table = stage2, land3, own3, change, table
        self.s_core, self.s_y, self.s_z = link.slots(NY), link.slots(2 * NY), link.slots(NZ)
        self.g_z, self.g_y, self.g_core = link.slots(NZ), link.slots(NY * TILES), link.slots(NY)

    def to_core(self):
        h = self.here
        for k in range(1, NY + 1):
            i = h.ys.at(k)
            self.link.start(self.part.at[i], self.land1.at[i], self.s_core + i, self.s_core + i, h.other)

    def to_y(self):
        h = self.here
        for k in range(1, NY + 1):
            i = h.ys.at(k)
            self.link.arrived(self.land1.at[i], self.s_core + i, h.other)
            total = self.own1[i] + self.land1[i].astype(F32)
            if k == NY:
                self.own2[...] = total
            else:
                self.stage1[i] = rounded(total)
        for g, columns in enumerate((pl.ds(0, LEFT), pl.ds(LEFT, HALF))):
            for k in (2, 1, 3):
                i = h.ys.at(k)
                self.link.start(
                    self.stage1.at[i, :, :, columns], self.land2.at[h.y, :, :, columns],
                    self.s_y + 2 * i + g, self.s_y + 2 * h.y + g, h.ys.peer(i),
                )

    def to_z(self):
        h = self.here
        counts = []
        for g, columns in enumerate((pl.ds(0, LEFT), pl.ds(LEFT, HALF))):
            for k in range(1, NY):
                i = h.ys.back(k)
                self.link.arrived(self.land2.at[i, :, :, columns], self.s_y + 2 * i + g, h.ys.peer(i))
            for r in range(TILES):
                total = self.own2[r, :, columns]
                for k in range(1, NY):
                    total = total + self.land2[h.ys.back(k), r, :, columns].astype(F32)
                if g == 0:
                    counts.append(total[:, :LANES])
                else:
                    total = jnp.concatenate([counts[r], total], axis=1)
                j = 2 * r + g
                self.stage2[j] = rounded(total)

                @pl.when(h.z == j)
                def _():
                    self.own3[...] = total

                self.link.start(
                    self.stage2.at[j], self.land3.at[h.z], self.s_z + j, self.s_z + h.z, h.zs.peer(j), h.z != j
                )

    def piece(self, j):
        side = pl.multiple_of(lax.rem(j, 2) * HALF, LANES)
        return self.table.at[self.here.c, self.here.y, j // 2, :, pl.ds(side, HALF)]

    def update(self):
        h = self.here
        total = self.own3[...]
        for k in range(1, NZ):
            j = h.zs.back(k)
            self.link.arrived(self.land3.at[j], self.s_z + j, h.zs.peer(j))
            total = total + self.land3[j].astype(F32)
        counts = both_parts(total[:, :LANES])[:, :1]
        fresh = 0.5 * self.change[...] + 0.5 * (total[:, LANES:] / (counts + 1.0))
        self.change[...] = fresh
        for side in range(2):

            @pl.when(lax.rem(h.z, 2) == side)
            def _():
                self.table[h.c, h.y, h.z // 2, :, side * HALF : (side + 1) * HALF] = fresh.astype(BF16)

        mine = self.piece(h.z)
        for k in (4, 3, 5, 2, 6, 1, 7):
            j = h.zs.at(k)
            self.link.start(mine, mine, self.g_z + j, self.g_z + h.z, h.zs.peer(j))

    def gather_y(self):
        h = self.here
        for m in (0, 1, 3, 2):
            p = lax.rem(h.z // 2 + m, TILES)
            for j in [h.z + 1 - 2 * lax.rem(h.z, 2)] if m == 0 else [2 * p, 2 * p + 1]:
                self.link.arrived(self.piece(j), self.g_z + j, h.zs.peer(j))
            mine = self.table.at[h.c, h.y, p]
            for k in (2, 1, 3):
                i = h.ys.at(k)
                self.link.start(mine, mine, self.g_y + TILES * i + p, self.g_y + TILES * h.y + p, h.ys.peer(i))
        mine = self.table.at[h.c, h.y]
        self.link.start(mine, mine, self.g_core + h.y, self.g_core + h.y, h.other)

    def gather_core(self):
        h = self.here
        for k in (1, 3, 2):
            i = h.ys.back(k)
            for p in range(TILES):
                self.link.arrived(self.table.at[h.c, i, p], self.g_y + TILES * i + p, h.ys.peer(i))
            here = self.table.at[h.c, i]
            self.link.start(here, here, self.g_core + i, self.g_core + i, h.other)

    def gathered(self):
        h = self.here
        for i in range(NY):
            self.link.arrived(self.table.at[1 - h.c, i], self.g_core + i, h.other)


class Route:
    def __init__(self, here, link, src, near, middle, got, mix=None):
        self.here, self.link = here, link
        self.src, self.near, self.middle, self.got, self.mix = src, near, middle, got, mix
        self.s_core, self.s_y, self.s_z = link.slots(1), link.slots(2 * NY), link.slots(NZ)

    def to_core(self):
        h = self.here
        self.link.start(self.src.at[1 - h.c], self.near, self.s_core, self.s_core, h.other)

    def to_y(self):
        h = self.here
        self.link.arrived(self.near, self.s_core, h.other)
        for s, ref in enumerate((self.src.at[h.c], self.near)):
            for k in (2, 1, 3):
                i = h.ys.at(k)
                self.link.start(
                    ref.at[i], self.middle.at[h.y, s], self.s_y + 2 * i + s, self.s_y + 2 * h.y + s, h.ys.peer(i)
                )
            self.middle[h.y, s] = ref[h.y]

    def to_z(self):
        h = self.here
        for k in range(1, NY):
            i = h.ys.back(k)
            for s in range(2):
                self.link.arrived(self.middle.at[i, s], self.s_y + 2 * i + s, h.ys.peer(i))
        if self.mix is None:
            blocks = lambda j: self.middle.at[:, :, j]
        else:
            d, s = iota((SENDS, SENDS), 0), iota((SENDS, SENDS), 1)
            order = (s == ((d & 31) >> 2) * 32 + (d >> 5) * 4 + (d & 3)).astype(BF16)
            mixed = dot(order, self.middle[...].reshape(SENDS, WIDE)).astype(BF16)
            self.mix[...] = mixed.reshape(self.mix.shape)
            blocks = lambda j: self.mix.at[j]
        for k in (4, 3, 5, 2, 6, 1, 7):
            j = h.zs.at(k)
            self.link.start(blocks(j), self.got.at[h.z], self.s_z + j, self.s_z + h.z, h.zs.peer(j))
        self.got[h.z] = blocks(h.z)[...]

    def finish(self):
        h = self.here
        for k in range(1, NZ):
            j = h.zs.back(k)
            self.link.arrived(self.got.at[j], self.s_z + j, h.zs.peer(j))


def whole_kernel(
    corpus_ref, c0_ref, cand_ref, leaf_ref, slots_ref,
    table_ref, total_ref, count_ref,
    part, own1, land1, stage1, land2, own2, stage2, land3, own3, change, table1,
    norm_ref, comp_ref, pick_ref, wsend, wnear, wmiddle, wgot, csend, cnear, cmiddle, cmix, cgot,
    pairs_ref, sums_ref, lands_ref, send, recv,
):
    h = Here()
    greeted = h.greet()
    link = Link(send, recv)
    chunks = []
    for n in range(4):
        t = n % CHUNKS
        table = (table1 if n < CHUNKS else table_ref).at[t]
        refs = [r.at[n] for r in (part, own1, land1, stage1, land2, own2, stage2, land3, own3)]
        chunks.append(Chunk(h, link, *refs, change.at[t], table))
    weights_route = Route(h, link, wsend, wnear, wmiddle, wgot)
    corpus_route = Route(h, link, csend, cnear, cmiddle, cgot, cmix)
    cand = in_lanes(cand_ref) - h.x * (CENTS // BLOCK)
    norm_ref[...] = row_norms(corpus_ref[...])
    change[...] = jnp.zeros_like(change)
    comp_ref[...] = jnp.zeros_like(comp_ref)

    def compute(n, core):
        t = n % CHUNKS
        cents = c0_ref[t, core]
        if n >= CHUNKS:
            cents = 0.5 * cents + table1[t, core].reshape(TILE, D).astype(F32)
        corpus = corpus_ref[...]
        first = (t * NC + core) * (TILE // BLOCK)
        weights, compact = tile_weights(cents, corpus, norm_ref[...], cand, first)
        if n >= CHUNKS:
            comp_ref[...] += compact
        counts = jnp.sum(weights.astype(F32), axis=1, keepdims=True)
        counts = encode_counts(jnp.broadcast_to(counts, (TILE, LANES)))
        sums = dot(weights, corpus)
        return jnp.concatenate([counts, sums], axis=1).reshape(NY, TILES, 16, WIDE)

    def far(n):
        chunks[n].part[...] = compute(n, 1 - h.c).astype(BF16)

    def near(n):
        chunks[n].own1[...] = compute(n, h.c)

    far(0)
    greeted()
    chunks[0].to_core()
    near(0)
    chunks[0].to_y()
    far(1)
    chunks[1].to_core()
    near(1)
    chunks[1].to_y()

    owner, slot, rank = positions(in_lanes(leaf_ref), slots_ref[...])
    spot = ((owner & 1) * NY + ((owner >> 1) & 3)) * NZ + (owner >> 3)
    quarter = iota((1, ROWS), 1) >> 8
    fill = iota((BLOCK, ROWS), 0)
    meta = jnp.where(fill == 0, slot, jnp.where(fill == 1, cand.astype(F32), 0.0))
    short = jnp.where(quarter == h.x, spot * 4 + rank, -1)
    whole = (iota((SENDS, ROWS), 0) == short).astype(BF16)
    folded = whole[:, :SENDS] + whole[:, SENDS : 2 * SENDS] + whole[:, 2 * SENDS : 3 * SENDS] + whole[:, 3 * SENDS :]
    mine = corpus_ref[pl.ds(pl.multiple_of(h.x * SENDS, SENDS), SENDS), :]
    marks = dot(whole, jnp.concatenate([jnp.zeros((BLOCK, ROWS), F32), meta], axis=0).astype(BF16), 1, 1)
    rows = jnp.concatenate([dot(folded, mine), marks], axis=1).astype(BF16)
    csend[...] = rows.reshape(csend.shape)
    target = spot * 16 + quarter * 4 + rank
    for t in range(ROWS // TILE):
        pick_ref[t * TILE : (t + 1) * TILE, :] = (iota((TILE, ROWS), 0) + t * TILE == target).astype(BF16)
    corpus_route.to_core()

    chunks[0].to_z()
    chunks[1].to_z()
    chunks[0].update()
    corpus_route.to_y()
    chunks[1].update()
    chunks[0].gather_y()
    chunks[1].gather_y()
    chunks[0].gather_core()
    near(2)
    chunks[0].gathered()
    far(2)
    chunks[2].to_core()
    chunks[1].gather_core()
    corpus_route.to_z()
    chunks[2].to_y()
    near(3)
    chunks[1].gathered()
    far(3)
    chunks[3].to_core()
    chunks[3].to_y()
    load = jnp.concatenate([comp_ref[...], meta], axis=0).astype(BF16)
    for s in range(NC):
        half = dot(pick_ref[s * ROWS // 2 : (s + 1) * ROWS // 2, :], load, 1, 1).astype(BF16)
        wsend[s] = half.reshape(wsend.shape[1:])
    weights_route.to_core()
    chunks[2].to_z()
    weights_route.to_y()
    chunks[3].to_z()
    chunks[2].update()
    chunks[3].update()
    weights_route.to_z()
    chunks[2].gather_y()
    chunks[3].gather_y()

    corpus_route.finish()
    eye = (iota((LANES, LANES), 0) == iota((LANES, LANES), 1)).astype(BF16)
    came = cgot[...].reshape(SENDS, WIDE)
    turned = dot(eye, came[:, D:], 1, 1)
    chosen = (iota((LEAF_DEV, SENDS), 0) == turned[BLOCK : BLOCK + 1].astype(jnp.int32)).astype(BF16)
    sums = dot(chosen, came[:, :D])
    chunks[2].gather_core()
    weights_route.finish()
    turned = dot(eye, wgot[...].reshape(ROWS, LANES), 1, 1)
    weights, slot, block = turned[:BLOCK], turned[BLOCK : BLOCK + 1], turned[BLOCK + 1 : BLOCK + 2]
    chosen = jnp.where(iota((LEAF_DEV, ROWS), 0) == slot.astype(jnp.int32), 1.0, 0.0)
    counts = jnp.broadcast_to(jnp.sum(chosen, axis=1, keepdims=True), (LEAF_DEV, LANES))
    pairs_ref[...] = counts.reshape(pairs_ref.shape)
    count_ref[...] = pairs_ref[h.x]
    chosen = chosen.astype(BF16)
    mixed = []
    for b in range(0, CENTS // BLOCK, 2):
        both = jnp.concatenate([jnp.where(block == b + s, weights, 0.0) for s in range(2)], axis=0)
        mixed.append(dot(chosen, both.astype(BF16), 1, 1))
    chunks[3].gather_core()
    for t in range(CHUNKS):
        chunks[CHUNKS + t].gathered()
        for core in range(NC):
            half = (0.25 * c0_ref[t, core] + table_ref[t, core].reshape(TILE, D).astype(F32)).astype(BF16)
            first = (t * NC + core) * 2
            high_low = jnp.concatenate(mixed[first : first + 2], axis=1)
            high = high_low.astype(BF16)
            low = (high_low - high.astype(F32)).astype(BF16)
            sums = sums - (dot(high, half) + dot(low, half))
    sums_ref[...] = sums.reshape(sums_ref.shape)
    s_x = link.slots(NX)
    for k in range(1, NX):
        i = h.xs.at(k)
        link.start(sums_ref.at[i], lands_ref.at[h.x], s_x + i, s_x + h.x, h.xs.peer(i))
    total = sums_ref[h.x]
    for k in range(1, NX):
        i = h.xs.back(k)
        link.arrived(lands_ref.at[i], s_x + i, h.xs.peer(i))
        total = total + lands_ref[i]
    total_ref[...] = total
    link.finish()


def on_device(corpus, initial_centroids, cand_block, leaf_ids, slot_table):
    per = LEAF_DEV // NX
    four = 2 * CHUNKS
    block = (NY, TILES, 16, WIDE)
    scratch = [
        pltpu.VMEM((four, *block), BF16),
        pltpu.VMEM((four, *block), F32),
        pltpu.VMEM((four, *block), BF16),
        pltpu.VMEM((four, *block), BF16),
        pltpu.VMEM((four, *block), BF16),
        pltpu.VMEM((four, *block[1:]), F32),
        pltpu.VMEM((four, NZ, 16, LEFT), BF16),
        pltpu.VMEM((four, NZ, 16, LEFT), BF16),
        pltpu.VMEM((four, 16, LEFT), F32),
        pltpu.VMEM((CHUNKS, 16, HALF), F32),
        pltpu.VMEM((CHUNKS, NC, NY, TILES, 16, D), BF16),
        pltpu.VMEM((1, ROWS), F32),
        pltpu.VMEM((BLOCK, ROWS), F32),
        pltpu.VMEM((ROWS, ROWS), BF16),
        pltpu.VMEM((NC, NY, NZ, 16, LANES), BF16),
        pltpu.VMEM((NY, NZ, 16, LANES), BF16),
        pltpu.VMEM((NY, NC, NZ, 16, LANES), BF16),
        pltpu.VMEM((NZ, NY, NC, 16, LANES), BF16),
        pltpu.VMEM((NC, NY, 32, WIDE), BF16),
        pltpu.VMEM((NY, 32, WIDE), BF16),
        pltpu.VMEM((NY, NC, 32, WIDE), BF16),
        pltpu.VMEM((NZ, 32, WIDE), BF16),
        pltpu.VMEM((NZ, 32, WIDE), BF16),
        pltpu.VMEM((NX, per, LANES), F32),
        pltpu.VMEM((NX, per, D), F32),
        pltpu.VMEM((NX, per, D), F32),
        pltpu.SemaphoreType.DMA((SEMAPHORES,)),
        pltpu.SemaphoreType.DMA((SEMAPHORES,)),
    ]
    change, total, count = pl.pallas_call(
        whole_kernel,
        out_shape=[
            jax.ShapeDtypeStruct((CHUNKS, NC, NY, TILES, 16, D), BF16),
            jax.ShapeDtypeStruct((per, D), F32),
            jax.ShapeDtypeStruct((per, LANES), F32),
        ],
        in_specs=[ANYWHERE] * 5,
        out_specs=[ANYWHERE] * 3,
        scratch_shapes=scratch,
        compiler_params=pltpu.CompilerParams(collective_id=1, has_side_effects=True, vmem_limit_bytes=LIMIT),
        name="whole",
    )(
        corpus,
        initial_centroids.reshape(CHUNKS, NC, TILE, D),
        cand_block.reshape(-1, LANES),
        leaf_ids.reshape(-1, LANES),
        slot_table.reshape(-1, LANES),
    )
    centroids = 0.25 * initial_centroids + change.reshape(CENTS, D).astype(F32)
    return centroids, total / (count[:, :1] + 1.0)


def solution(mesh):
    in_specs = (P("rows", None), P("rep", None), P("rows"), P("rows"), P())
    out_specs = (P("rep", None), P(("rows", "rep"), None))
    return jax.shard_map(
        on_device, mesh=mesh, in_specs=in_specs, out_specs=out_specs, check_vma=False
    )
```

```python
import functools

import jax
import jax.numpy as jnp
from jax import lax
from jax.experimental import pallas as pl
from jax.experimental.pallas import tpu as pltpu
from jax.sharding import PartitionSpec as P

D = 768
BLOCK = 64
LANES = 128
WIDE = D + LANES
NZ, NY, NC, NX = 8, 4, 2, 4
OWNERS = NZ * NY * NC
ROWS = 1024
CENTS = 1024
SENDS = 256
TILE = 256
LEAF_DEV = 64
CHUNKS, TILES = 4, 2
SIDES = 3
SIDE = D // SIDES
PIECES = TILES * SIDES
OWN, AWAY, NEAR, CHIP, RING, FROM_Y = range(6)
FROM_Z = FROM_Y + NY
F32, BF16 = jnp.float32, jnp.bfloat16
MESH = pl.DeviceIdType.MESH
ANYWHERE = pl.BlockSpec(memory_space=pltpu.VMEM)
LIMIT = 56 * 1024 * 1024
SEMAPHORES = CHUNKS * (6 + TILES + NY + 1) + 2 * 3 + 1
ORDER = (
    "K0 K1 Y0 K2", "Y1 K3 Y2 Y3", "Z0 P Z1 Z2", "U0 Z3 c1 U1", "U2 G0 U3 G1", "c2 G2 H0 W0",
    "K4 G3 H1 Y4", "W1 K5 H2 Y5", "W2 K6 H3 Y6", "Z4 W3 K7 Y7", "Z5 Q Z6 U4", "Z7 w1 U5 G4",
    "U6 U7 G5 w2", "G6 H4 G7 S", "H5 H6 W4 W5", "R L4 L5 H7", "W6 L6 W7 L7",
)


def iota(shape, axis):
    return lax.broadcasted_iota(jnp.int32, shape, axis)


def dot(a, b, ca=1, cb=0):
    return lax.dot_general(a, b, (((ca,), (cb,)), ((), ())), preferred_element_type=F32)


def place():
    r = lax.axis_index("rows")
    return r // (NY * NC), lax.rem(r // NC, NY), lax.rem(r, NC), lax.axis_index("rep")


def row_index(z, y, c):
    return (z * NY + y) * NC + c


def row_norms(corpus):
    square = jnp.square(corpus.astype(F32))
    high = square.astype(BF16)
    low = (square - high.astype(F32)).astype(BF16)
    ones = jnp.ones((8, D), BF16)
    return (dot(ones, high, 1, 1) + dot(ones, low, 1, 1))[:1]


def tile_weights(cents, corpus, norms, cand, first_block):
    centre = jnp.sum(cents * cents, axis=1, keepdims=True)
    products = dot(cents.astype(BF16), corpus, 1, 1)
    kernel = 1.0 / (1.0 + (norms + centre - 2.0 * products) / D)
    parts, compact = [], None
    for b in range(TILE // BLOCK):
        piece = kernel[b * BLOCK : (b + 1) * BLOCK]
        total = jnp.sum(piece, axis=0, keepdims=True)
        piece = jnp.where(cand == first_block + b, piece / total, 0.0).astype(BF16)
        parts.append(piece)
        wide = piece.astype(F32)
        compact = wide if compact is None else compact + wide
    return jnp.concatenate(parts, axis=0), compact


def in_lanes(ref):
    values = ref[...]
    return jnp.concatenate([values[i : i + 1] for i in range(values.shape[0])], axis=1)


def positions(leaf, slots):
    upper = (iota((slots.shape[0], ROWS), 0) == (leaf >> 7)).astype(BF16)
    lower = iota((slots.shape[1], ROWS), 0) == (leaf & 127)

    def look(values):
        found = dot(values.astype(F32).astype(BF16), upper, 0, 0)
        return jnp.sum(jnp.where(lower, found, 0.0), axis=0, keepdims=True)

    owner, slot = look(slots >> 6).astype(jnp.int32), look(slots & 63)
    hits = iota((OWNERS, ROWS), 0) == owner
    before = (iota((SENDS, SENDS), 0) < iota((SENDS, SENDS), 1)).astype(BF16)
    ranks = []
    for q in range(ROWS // SENDS):
        own = hits[:, q * SENDS : (q + 1) * SENDS]
        ahead = dot(jnp.where(own, 1.0, 0.0).astype(BF16), before)
        ranks.append(jnp.sum(jnp.where(own, ahead, 0.0), axis=0, keepdims=True))
    return owner, slot, jnp.concatenate(ranks, axis=1).astype(jnp.int32)


class Link:
    def __init__(self, send, recv):
        self.send, self.recv, self.used, self.sent = send, recv, 0, []

    def slots(self, count):
        first = self.used
        self.used += count
        return first

    def make(self, src, dst, out, into, device):
        return pltpu.make_async_remote_copy(
            src_ref=src, dst_ref=dst, send_sem=self.send.at[out], recv_sem=self.recv.at[into],
            device_id=device, device_id_type=MESH,
        )

    def start(self, src, dst, slot, device, into=None):
        self.make(src, dst, slot, slot if into is None else into, device).start()

    def arrived(self, whole, slot, device):
        self.make(whole, whole, slot, slot, device).wait_recv()

    def sends(self, whole, slot, device, when=None):
        self.sent.append((self.make(whole, whole, slot, slot, device), when))

    def finish(self):
        for copy, when in self.sent:
            if when is None:
                copy.wait_send()
            else:
                pl.when(when)(copy.wait_send)
        self.sent.clear()


class Axis:
    def __init__(self, size, me, peer):
        self.size, self.me, self.peer = size, me, peer

    def at(self, k):
        return lax.rem(self.me + k, self.size)

    def back(self, k):
        return lax.rem(self.me + self.size - k, self.size)


class Here:
    def __init__(self):
        z, y, c, x = place()
        self.z, self.y, self.c, self.x = z, y, c, x
        row = row_index(z, y, c)
        self.zs = Axis(NZ, z, lambda i: (row_index(i, y, c), x))
        self.ys = Axis(NY, y, lambda i: (row_index(z, i, c), x))
        self.xs = Axis(NX, x, lambda i: (row, i))
        self.other = (row_index(z, y, 1 - c), x)

    def greet(self):
        barrier = pltpu.get_barrier_semaphore()
        peers = [self.other] + [a.peer(a.at(k)) for a in (self.zs, self.ys, self.xs) for k in range(1, a.size)]
        for peer in peers:
            pl.semaphore_signal(barrier, inc=1, device_id=peer, device_id_type=MESH)
        return lambda: pl.semaphore_wait(barrier, len(peers))


class Chunk:
    def __init__(self, here, link, base, t, part, own1, land1, stage1, land2, own2, stage2, land3, own3, counts, change, table):
        self.here, self.link, self.t = here, link, t
        self.part, self.own1, self.land1, self.stage1, self.land2, self.own2 = part, own1, land1, stage1, land2, own2
        self.stage2, self.land3, self.own3, self.counts, self.change, self.table = stage2, land3, own3, counts, change, table
        self.c_core, self.c_y, self.c_z, self.s_core, self.s_y, self.s_z = range(base, base + 6)
        self.g_z, self.g_y, self.g_core = base + 6, base + 6 + TILES, base + 6 + TILES + NY
        self.owners = [(j + 2 * t) % NZ for j in range(PIECES)]
        self.index = lax.rem(here.z + (NZ - 2 * t), NZ)
        self.owns = self.index < PIECES

    def to_core(self):
        h = self.here
        self.link.start(self.counts.at[AWAY], self.counts.at[NEAR], self.c_core, h.other)
        self.link.start(self.part, self.land1, self.s_core, h.other)
        self.link.sends(self.counts.at[AWAY], self.c_core, h.other)
        self.link.sends(self.part, self.s_core, h.other)

    def to_y(self):
        h = self.here
        self.link.arrived(self.counts.at[NEAR], self.c_core, h.other)
        self.counts[CHIP] = self.counts[OWN] + self.counts[NEAR]
        for k in (2, 1, 3):
            self.link.start(self.counts.at[CHIP], self.counts.at[FROM_Y + h.y], self.c_y, h.ys.peer(h.ys.at(k)))
        self.link.arrived(self.land1, self.s_core, h.other)
        for k in (2, 1, 3):
            i = h.ys.at(k)
            self.stage1[i] = (self.own1[i] + self.land1[i].astype(F32)).astype(BF16)
            self.link.start(self.stage1.at[i], self.land2.at[h.y], self.s_y, h.ys.peer(i))
        self.own2[...] = self.own1[h.y] + self.land1[h.y].astype(F32)
        self.link.sends(self.counts.at[pl.ds(FROM_Y, NY - 1)], self.c_y, h.other)
        self.link.sends(self.stage1.at[pl.ds(0, NY - 1)], self.s_y, h.other)

    def to_z(self):
        h = self.here
        counts = self.counts[CHIP]
        self.link.arrived(self.counts.at[pl.ds(FROM_Y, NY - 1)], self.c_y, h.other)
        for k in range(1, NY):
            counts = counts + self.counts[FROM_Y + h.ys.back(k)]
        self.counts[RING] = counts
        for owner in self.owners:

            @pl.when(h.z != owner)
            def _():
                self.link.start(self.counts.at[RING], self.counts.at[FROM_Z + h.z], self.c_z, h.zs.peer(owner))

        self.link.arrived(self.land2.at[pl.ds(0, NY - 1)], self.s_y, h.other)
        for j, owner in enumerate(self.owners):
            r, columns = j // SIDES, slice(j % SIDES * SIDE, (j % SIDES + 1) * SIDE)
            total = self.own2[r, :, columns]
            for k in range(1, NY):
                total = total + self.land2[h.ys.back(k), r, :, columns].astype(F32)
            self.stage2[j] = total.astype(BF16)

            @pl.when(h.z == owner)
            def _():
                self.own3[...] = total

            @pl.when(h.z != owner)
            def _():
                self.link.start(self.stage2.at[j], self.land3.at[h.z], self.s_z, h.zs.peer(owner))

        for count, when in ((PIECES - 1, self.owns), (PIECES, jnp.logical_not(self.owns))):
            self.link.sends(self.counts.at[pl.ds(FROM_Z, count)], self.c_z, h.other, when)
            self.link.sends(self.stage2.at[pl.ds(0, count)], self.s_z, h.other, when)

    def piece(self, index):
        side = pl.multiple_of(lax.rem(index, SIDES) * SIDE, LANES)
        return self.table.at[self.here.c, self.here.y, index // SIDES, :, pl.ds(side, SIDE)]

    def update(self):
        h = self.here
        self.link.sends(self.land3.at[pl.ds(0, NZ - 1)], self.g_z, h.other, self.owns)

        @pl.when(self.owns)
        def _():
            tally, total = self.counts[RING], self.own3[...]
            self.link.arrived(self.counts.at[pl.ds(FROM_Z, NZ - 1)], self.c_z, h.other)
            self.link.arrived(self.land3.at[pl.ds(0, NZ - 1)], self.s_z, h.other)
            for k in range(1, NZ):
                j = h.zs.back(k)
                tally = tally + self.counts[FROM_Z + j]
                total = total + self.land3[j].astype(F32)
            tile = self.index // SIDES
            lane = h.y * 32 + tile * 16
            found = iota((16, LANES), 1) == lane + iota((16, LANES), 0)
            counts = jnp.sum(jnp.where(found, tally, 0.0), axis=1, keepdims=True)
            fresh = 0.5 * self.change[...] + 0.5 * (total / (counts + 1.0))
            self.change[...] = fresh
            mine = self.piece(self.index)
            mine[...] = fresh.astype(BF16)
            for k in (4, 3, 5, 2, 6, 1, 7):
                self.link.start(mine, mine, self.g_z, h.zs.peer(h.zs.at(k)), self.g_z + tile)

    def gather_y(self):
        h = self.here
        for r in range(TILES):
            mine = self.table.at[h.c, h.y, r]
            own = jnp.logical_and(self.owns, self.index // SIDES == r)

            @pl.when(own)
            def _():
                self.link.arrived(mine.at[:, pl.ds(0, D - SIDE)], self.g_z + r, h.other)

            @pl.when(jnp.logical_not(own))
            def _():
                self.link.arrived(mine, self.g_z + r, h.other)

            for k in (2, 1, 3):
                self.link.start(mine, mine, self.g_y, h.ys.peer(h.ys.at(k)), self.g_y + k)
        mine = self.table.at[h.c, h.y]
        self.link.start(mine, mine, self.g_core, h.other)
        self.link.sends(self.table.at[h.c, pl.ds(0, NY - 1)], self.g_y, h.other)

    def gather_core(self):
        h = self.here
        for k in (1, 3, 2):
            here = self.table.at[h.c, h.ys.back(k)]
            self.link.arrived(here, self.g_y + k, h.other)
            self.link.start(here, here, self.g_core, h.other)
        self.link.sends(self.table.at[h.c], self.g_core, h.other)

    def gathered(self):
        self.link.arrived(self.table.at[1 - self.here.c], self.g_core, self.here.other)


class Route:
    def __init__(self, here, link, src, near, middle, got, mix=None):
        self.here, self.link = here, link
        self.src, self.near, self.middle, self.got, self.mix = src, near, middle, got, mix
        self.s_core, self.s_y, self.s_z = link.slots(1), link.slots(1), link.slots(1)

    def to_core(self):
        h = self.here
        self.link.start(self.src.at[1 - h.c], self.near, self.s_core, h.other)
        self.link.sends(self.near, self.s_core, h.other)

    def to_y(self):
        h = self.here
        self.link.arrived(self.near, self.s_core, h.other)
        for s, ref in enumerate((self.src.at[h.c], self.near)):
            for k in (2, 1, 3):
                i = h.ys.at(k)
                self.link.start(ref.at[i], self.middle.at[h.y, s], self.s_y, h.ys.peer(i))
            self.middle[h.y, s] = ref[h.y]
        self.link.sends(self.middle.at[pl.ds(0, NY - 1)], self.s_y, h.other)

    def to_z(self):
        h = self.here
        self.link.arrived(self.middle.at[pl.ds(0, NY - 1)], self.s_y, h.other)
        if self.mix is None:
            blocks = lambda j: self.middle.at[:, :, j]
        else:
            d, s = iota((SENDS, SENDS), 0), iota((SENDS, SENDS), 1)
            order = (s == ((d & 31) >> 2) * 32 + (d >> 5) * 4 + (d & 3)).astype(BF16)
            mixed = dot(order, self.middle[...].reshape(SENDS, WIDE)).astype(BF16)
            self.mix[...] = mixed.reshape(self.mix.shape)
            blocks = lambda j: self.mix.at[j]
        for k in (4, 3, 5, 2, 6, 1, 7):
            j = h.zs.at(k)
            self.link.start(blocks(j), self.got.at[h.z], self.s_z, h.zs.peer(j))
        self.got[h.z] = blocks(h.z)[...]
        self.link.sends(self.got.at[pl.ds(0, NZ - 1)], self.s_z, h.other)

    def finish(self):
        self.link.arrived(self.got.at[pl.ds(0, NZ - 1)], self.s_z, self.here.other)


def whole_kernel(
    corpus_any, c0_any, cand_ref, leaf_ref, slots_ref,
    table_any, own_ref, away1, away2, away3, count_ref,
    part, own1, land1, stage1, land2, own2, stage2, land3, own3, counts, change, table1, table2,
    corpus_ref, c0_ref, norm_ref, comp_ref, pick_ref, mixed_ref,
    wsend, wnear, wmiddle, wgot, rsend, rnear, rmiddle, rmix, rgot,
    share_ref, sums_ref, lands_ref, send, recv, fetch,
):
    h = Here()
    fetches = [pltpu.make_async_copy(corpus_any, corpus_ref, fetch.at[CHUNKS])]
    fetches += [pltpu.make_async_copy(c0_any.at[t], c0_ref.at[t], fetch.at[t]) for t in range(CHUNKS)]
    for copy in fetches[:2]:
        copy.start()
    greeted = h.greet()
    links = [Link(send, recv) for _ in range(CHUNKS + 1)]
    link = links[CHUNKS]
    bases = [link.slots(7 + TILES + NY) for _ in range(CHUNKS)]
    chunks = []
    for n in range(2 * CHUNKS):
        t = n % CHUNKS
        table = (table1 if n < CHUNKS else table2).at[t]
        refs = [r.at[n] for r in (part, own1, land1, stage1, land2, own2, stage2, land3, own3, counts)]
        chunks.append(Chunk(h, links[t], bases[t], t, *refs, change.at[t], table))
    weights_route = Route(h, link, wsend, wnear, wmiddle, wgot)
    corpus_route = Route(h, link, rsend, rnear, rmiddle, rgot, rmix)
    s_x = link.slots(1)
    cand = in_lanes(cand_ref) - h.x * (CENTS // BLOCK)
    change[...] = jnp.zeros_like(change)
    comp_ref[...] = jnp.zeros_like(comp_ref)
    fetches[0].wait()
    for copy in fetches[2:]:
        copy.start()
    norm_ref[...] = row_norms(corpus_ref[...])
    meta, stores = [], []

    def compute(n):
        t = n % CHUNKS
        if n < CHUNKS:
            fetches[1 + t].wait()
        cents = c0_ref[t]
        if n >= CHUNKS:
            cents = 0.5 * cents + table1[t].reshape(TILE, D).astype(F32)
        corpus = corpus_ref[...]
        weights, compact = tile_weights(cents, corpus, norm_ref[...], cand, t * (TILE // BLOCK))
        if n >= CHUNKS:
            comp_ref[...] += compact
        tally = dot(jnp.ones((8, ROWS), BF16), weights, 1, 1)
        left, right = tally[:1, :LANES], tally[:1, LANES:]
        chunks[n].counts[OWN] = jnp.where(h.c == 0, left, right)
        chunks[n].counts[AWAY] = jnp.where(h.c == 0, right, left)
        sums = dot(weights, corpus).reshape(NC, NY, TILES, 16, D)
        for s in range(NC):

            @pl.when(h.c == s)
            def _():
                chunks[n].own1[...] = sums[s]

            @pl.when(h.c != s)
            def _():
                chunks[n].part[...] = sums[s].astype(BF16)

        if n >= CHUNKS:
            links[t].finish()
        if n == 0:
            greeted()
        chunks[n].to_core()

    def prepare():
        owner, slot, rank = positions(in_lanes(leaf_ref), slots_ref[...])
        spot = ((owner & 1) * NY + ((owner >> 1) & 3)) * NZ + (owner >> 3)
        quarter = iota((1, ROWS), 1) >> 8
        fill = iota((BLOCK, ROWS), 0)
        meta.append(jnp.where(fill == 0, slot, jnp.where(fill == 1, cand.astype(F32), 0.0)))
        short = jnp.where(quarter == h.x, spot * 4 + rank, -1)
        whole = (iota((SENDS, ROWS), 0) == short).astype(BF16)
        folded = whole[:, :SENDS] + whole[:, SENDS : 2 * SENDS] + whole[:, 2 * SENDS : 3 * SENDS] + whole[:, 3 * SENDS :]
        mine = corpus_ref[pl.ds(pl.multiple_of(h.x * SENDS, SENDS), SENDS), :]
        marks = dot(whole, jnp.concatenate([jnp.zeros((BLOCK, ROWS), F32), meta[0]], axis=0).astype(BF16), 1, 1)
        rows = jnp.concatenate([dot(folded, mine), marks], axis=1).astype(BF16)
        rsend[...] = rows.reshape(rsend.shape)
        target = spot * 16 + quarter * 4 + rank
        for t in range(ROWS // TILE):
            pick_ref[t * TILE : (t + 1) * TILE, :] = (iota((TILE, ROWS), 0) + t * TILE == target).astype(BF16)
        corpus_route.to_core()

    def send_weights():
        load = jnp.concatenate([comp_ref[...], meta[0]], axis=0).astype(BF16)
        for s in range(NC):
            half = dot(pick_ref[s * ROWS // 2 : (s + 1) * ROWS // 2, :], load, 1, 1).astype(BF16)
            wsend[s] = half.reshape(wsend.shape[1:])
        weights_route.to_core()

    def receive_corpus():
        eye = (iota((LANES, LANES), 0) == iota((LANES, LANES), 1)).astype(BF16)
        corpus_route.finish()
        came = rgot[...].reshape(SENDS, WIDE)
        turned = dot(eye, came[:, D:], 1, 1)
        chosen = (iota((LEAF_DEV, SENDS), 0) == turned[BLOCK : BLOCK + 1].astype(jnp.int32)).astype(BF16)
        sums_ref[...] = dot(chosen, came[:, :D]).reshape(sums_ref.shape)

    def receive_weights():
        eye = (iota((LANES, LANES), 0) == iota((LANES, LANES), 1)).astype(BF16)
        weights_route.finish()
        turned = dot(eye, wgot[...].reshape(ROWS, LANES), 1, 1)
        weights, slot, block = turned[:BLOCK], turned[BLOCK : BLOCK + 1], turned[BLOCK + 1 : BLOCK + 2]
        chosen = jnp.where(iota((LEAF_DEV, ROWS), 0) == slot.astype(jnp.int32), 1.0, 0.0)
        tally = jnp.broadcast_to(jnp.sum(chosen, axis=1, keepdims=True), (LEAF_DEV, LANES))
        share_ref[...] = tally.reshape(share_ref.shape)
        chosen = chosen.astype(BF16)
        for b in range(0, CENTS // BLOCK, 2):
            both = jnp.concatenate([jnp.where(block == b + s, weights, 0.0) for s in range(2)], axis=0)
            mixed_ref[b // 2] = dot(chosen, both.astype(BF16), 1, 1)

    def leaves(t):
        stores.append(pltpu.make_async_copy(table2.at[t], table_any.at[t], fetch.at[t]))
        stores[-1].start()
        cents = 0.25 * c0_ref[t] + table2[t].reshape(TILE, D).astype(F32)
        half = cents.astype(BF16)
        mixed = jnp.concatenate([mixed_ref[2 * t], mixed_ref[2 * t + 1]], axis=1)
        high = mixed.astype(BF16)
        low = (mixed - high.astype(F32)).astype(BF16)
        sums_ref[...] -= (dot(high, half) + dot(low, half)).reshape(sums_ref.shape)

    steps = dict(
        K=compute,
        Y=lambda n: chunks[n].to_y(),
        Z=lambda n: chunks[n].to_z(),
        U=lambda n: chunks[n].update(),
        G=lambda n: chunks[n].gather_y(),
        H=lambda n: chunks[n].gather_core(),
        W=lambda n: chunks[n].gathered(),
        L=lambda n: leaves(n - CHUNKS),
        c=lambda n: corpus_route.to_y() if n == 1 else corpus_route.to_z(),
        w=lambda n: weights_route.to_y() if n == 1 else weights_route.to_z(),
        P=lambda n: prepare(),
        Q=lambda n: send_weights(),
        R=lambda n: receive_weights(),
        S=lambda n: receive_corpus(),
    )
    for step in " ".join(ORDER).split():
        steps[step[0]](int(step[1:] or 0))
    own_ref[...] = sums_ref[h.x]
    for k, ref in enumerate((away1, away2, away3), 1):
        ref[...] = sums_ref[h.xs.at(k)]
    count_ref[...] = share_ref[h.x]
    for each in links:
        each.finish()
    for copy in stores:
        copy.wait()


def on_device(corpus, initial_centroids, cand_block, leaf_ids, slot_table):
    per = LEAF_DEV // NX
    steps = 2 * CHUNKS
    block = (NY, TILES, 16, D)
    scratch = [
        pltpu.VMEM((steps, *block), BF16),
        pltpu.VMEM((steps, *block), F32),
        pltpu.VMEM((steps, *block), BF16),
        pltpu.VMEM((steps, *block), BF16),
        pltpu.VMEM((steps, *block), BF16),
        pltpu.VMEM((steps, *block[1:]), F32),
        pltpu.VMEM((steps, PIECES, 16, SIDE), BF16),
        pltpu.VMEM((steps, NZ, 16, SIDE), BF16),
        pltpu.VMEM((steps, 16, SIDE), F32),
        pltpu.VMEM((steps, FROM_Z + NZ, 1, LANES), F32),
        pltpu.VMEM((CHUNKS, 16, SIDE), F32),
        pltpu.VMEM((CHUNKS, NC, *block), BF16),
        pltpu.VMEM((CHUNKS, NC, *block), BF16),
        pltpu.VMEM((ROWS, D), BF16),
        pltpu.VMEM((CHUNKS, TILE, D), F32),
        pltpu.VMEM((1, ROWS), F32),
        pltpu.VMEM((BLOCK, ROWS), F32),
        pltpu.VMEM((ROWS, ROWS), BF16),
        pltpu.VMEM((CENTS // LANES, LEAF_DEV, LANES), F32),
        pltpu.VMEM((NC, NY, NZ, 16, LANES), BF16),
        pltpu.VMEM((NY, NZ, 16, LANES), BF16),
        pltpu.VMEM((NY, NC, NZ, 16, LANES), BF16),
        pltpu.VMEM((NZ, NY, NC, 16, LANES), BF16),
        pltpu.VMEM((NC, NY, 32, WIDE), BF16),
        pltpu.VMEM((NY, 32, WIDE), BF16),
        pltpu.VMEM((NY, NC, 32, WIDE), BF16),
        pltpu.VMEM((NZ, 32, WIDE), BF16),
        pltpu.VMEM((NZ, 32, WIDE), BF16),
        pltpu.VMEM((NX, per, LANES), F32),
        pltpu.VMEM((NX, per, D), F32),
        pltpu.VMEM((NX, per, D), F32),
        pltpu.SemaphoreType.DMA((SEMAPHORES,)),
        pltpu.SemaphoreType.DMA((SEMAPHORES,)),
        pltpu.SemaphoreType.DMA((CHUNKS + 1,)),
    ]
    away = pl.BlockSpec(memory_space=pl.ANY)
    centroids, *sums, count = pl.pallas_call(
        whole_kernel,
        out_shape=[
            jax.ShapeDtypeStruct((CHUNKS, NC, *block), BF16),
            *[jax.ShapeDtypeStruct((per, D), F32)] * NX,
            jax.ShapeDtypeStruct((per, LANES), F32),
        ],
        in_specs=[away] * 2 + [ANYWHERE] * 3,
        out_specs=[away] + [ANYWHERE] * 5,
        scratch_shapes=scratch,
        compiler_params=pltpu.CompilerParams(collective_id=1, has_side_effects=True, vmem_limit_bytes=LIMIT),
        name="whole",
    )(
        corpus,
        initial_centroids.reshape(CHUNKS, TILE, D),
        cand_block.reshape(-1, LANES),
        leaf_ids.reshape(-1, LANES),
        slot_table.reshape(-1, LANES),
    )
    total = sums[0]
    for k in range(1, NX):
        total = total + lax.ppermute(sums[k], "rep", [(i, (i + k) % NX) for i in range(NX)])
    leaves = total / (count[:, :1] + 1.0)
    return 0.25 * initial_centroids + centroids.reshape(CENTS, D).astype(F32), leaves


def solution(mesh):
    in_specs = (P("rows", None), P("rep", None), P("rows"), P("rows"), P())
    out_specs = (P("rep", None), P(("rows", "rep"), None))
    return jax.shard_map(
        on_device, mesh=mesh, in_specs=in_specs, out_specs=out_specs, check_vma=False
    )
```

```python
import functools

import jax
import jax.numpy as jnp
from jax import lax
from jax.experimental import pallas as pl
from jax.experimental.pallas import tpu as pltpu
from jax.sharding import PartitionSpec as P

D = 768
BLOCK = 64
LANES = 128
WIDE = D + LANES
NZ, NY, NC, NX = 8, 4, 2, 4
OWNERS = NZ * NY * NC
ROWS = 1024
CENTS = 1024
SENDS = 256
TILE = 256
LEAF_DEV = 64
CHUNKS, TILES = 4, 2
SIDES = 3
SIDE = D // SIDES
PIECES = TILES * SIDES
OWN, AWAY, NEAR, CHIP, RING, FROM_Y = range(6)
FROM_Z = FROM_Y + NY
F32, BF16 = jnp.float32, jnp.bfloat16
MESH = pl.DeviceIdType.MESH
ANYWHERE = pl.BlockSpec(memory_space=pltpu.VMEM)
LIMIT = 56 * 1024 * 1024
SEMAPHORES = CHUNKS * (6 + TILES + NY + 1) + 2 * 3 + 1
ORDER = (
    "K0 K1 Y0 K2", "Y1 K3 Y2 Y3", "Z0 P Z1 Z2", "U0 Z3 c1 U1", "U2 G0 U3 G1", "c2 G2 H0 W0",
    "K4 G3 H1 Y4", "W1 K5 H2 Y5", "W2 K6 H3 Y6", "Z4 W3 K7 Y7", "Z5 Q Z6 U4", "Z7 w1 U5 G4",
    "U6 U7 w2 G5", "G6 H4 G7 S", "H5 H6 W4 W5", "H7 R L4 L5", "W6 L6 W7 L7",
)


def iota(shape, axis):
    return lax.broadcasted_iota(jnp.int32, shape, axis)


def dot(a, b, ca=1, cb=0):
    return lax.dot_general(a, b, (((ca,), (cb,)), ((), ())), preferred_element_type=F32)


def place():
    r = lax.axis_index("rows")
    return r // (NY * NC), lax.rem(r // NC, NY), lax.rem(r, NC), lax.axis_index("rep")


def row_index(z, y, c):
    return (z * NY + y) * NC + c


def row_norms(corpus):
    square = jnp.square(corpus.astype(F32))
    high = square.astype(BF16)
    low = (square - high.astype(F32)).astype(BF16)
    ones = jnp.ones((8, D), BF16)
    return (dot(ones, high, 1, 1) + dot(ones, low, 1, 1))[:1]


def tile_weights(cents, corpus, norms, cand, first_block):
    centre = jnp.sum(cents * cents, axis=1, keepdims=True)
    products = dot(cents.astype(BF16), corpus, 1, 1)
    kernel = 1.0 / (1.0 + (norms + centre - 2.0 * products) / D)
    parts, compact = [], None
    for b in range(TILE // BLOCK):
        piece = kernel[b * BLOCK : (b + 1) * BLOCK]
        total = jnp.sum(piece, axis=0, keepdims=True)
        piece = jnp.where(cand == first_block + b, piece / total, 0.0).astype(BF16)
        parts.append(piece)
        wide = piece.astype(F32)
        compact = wide if compact is None else compact + wide
    return jnp.concatenate(parts, axis=0), compact


def in_lanes(ref):
    values = ref[...]
    return jnp.concatenate([values[i : i + 1] for i in range(values.shape[0])], axis=1)


def positions(leaf, slots):
    upper = (iota((slots.shape[0], ROWS), 0) == (leaf >> 7)).astype(BF16)
    lower = iota((slots.shape[1], ROWS), 0) == (leaf & 127)

    def look(values):
        found = dot(values.astype(F32).astype(BF16), upper, 0, 0)
        return jnp.sum(jnp.where(lower, found, 0.0), axis=0, keepdims=True)

    owner, slot = look(slots >> 6).astype(jnp.int32), look(slots & 63)
    hits = iota((OWNERS, ROWS), 0) == owner
    before = (iota((SENDS, SENDS), 0) < iota((SENDS, SENDS), 1)).astype(BF16)
    ranks = []
    for q in range(ROWS // SENDS):
        own = hits[:, q * SENDS : (q + 1) * SENDS]
        ahead = dot(jnp.where(own, 1.0, 0.0).astype(BF16), before)
        ranks.append(jnp.sum(jnp.where(own, ahead, 0.0), axis=0, keepdims=True))
    return owner, slot, jnp.concatenate(ranks, axis=1).astype(jnp.int32)


class Link:
    def __init__(self, send, recv):
        self.send, self.recv, self.used, self.sent = send, recv, 0, []

    def slots(self, count):
        first = self.used
        self.used += count
        return first

    def make(self, src, dst, out, into, device):
        return pltpu.make_async_remote_copy(
            src_ref=src, dst_ref=dst, send_sem=self.send.at[out], recv_sem=self.recv.at[into],
            device_id=device, device_id_type=MESH,
        )

    def start(self, src, dst, slot, device, into=None):
        self.make(src, dst, slot, slot if into is None else into, device).start()

    def arrived(self, whole, slot, device):
        self.make(whole, whole, slot, slot, device).wait_recv()

    def sends(self, whole, slot, device, when=None):
        self.sent.append((self.make(whole, whole, slot, slot, device), when))

    def finish(self):
        for copy, when in self.sent:
            if when is None:
                copy.wait_send()
            else:
                pl.when(when)(copy.wait_send)
        self.sent.clear()


class Axis:
    def __init__(self, size, me, peer):
        self.size, self.me, self.peer = size, me, peer

    def at(self, k):
        return lax.rem(self.me + k, self.size)

    def back(self, k):
        return lax.rem(self.me + self.size - k, self.size)


class Here:
    def __init__(self):
        z, y, c, x = place()
        self.z, self.y, self.c, self.x = z, y, c, x
        row = row_index(z, y, c)
        self.zs = Axis(NZ, z, lambda i: (row_index(i, y, c), x))
        self.ys = Axis(NY, y, lambda i: (row_index(z, i, c), x))
        self.xs = Axis(NX, x, lambda i: (row, i))
        self.other = (row_index(z, y, 1 - c), x)

    def greet(self):
        barrier = pltpu.get_barrier_semaphore()
        peers = [self.other] + [a.peer(a.at(k)) for a in (self.zs, self.ys, self.xs) for k in range(1, a.size)]
        for peer in peers:
            pl.semaphore_signal(barrier, inc=1, device_id=peer, device_id_type=MESH)
        return lambda: pl.semaphore_wait(barrier, len(peers))


class Chunk:
    def __init__(self, here, link, base, t, part, own1, land1, stage1, land2, own2, stage2, land3, own3, counts, change, table):
        self.here, self.link, self.t = here, link, t
        self.part, self.own1, self.land1, self.stage1, self.land2, self.own2 = part, own1, land1, stage1, land2, own2
        self.stage2, self.land3, self.own3, self.counts, self.change, self.table = stage2, land3, own3, counts, change, table
        self.c_core, self.c_y, self.c_z, self.s_core, self.s_y, self.s_z = range(base, base + 6)
        self.g_z, self.g_y, self.g_core = base + 6, base + 6 + TILES, base + 6 + TILES + NY
        self.owners = [(j + 2 * t) % NZ for j in range(PIECES)]
        self.index = lax.rem(here.z + (NZ - 2 * t), NZ)
        self.owns = self.index < PIECES

    def to_core(self):
        h = self.here
        self.link.start(self.counts.at[AWAY], self.counts.at[NEAR], self.c_core, h.other)
        self.link.start(self.part, self.land1, self.s_core, h.other)
        self.link.sends(self.counts.at[AWAY], self.c_core, h.other)
        self.link.sends(self.part, self.s_core, h.other)

    def to_y(self):
        h = self.here
        self.link.arrived(self.counts.at[NEAR], self.c_core, h.other)
        self.counts[CHIP] = self.counts[OWN] + self.counts[NEAR]
        for k in (2, 1, 3):
            self.link.start(self.counts.at[CHIP], self.counts.at[FROM_Y + h.y], self.c_y, h.ys.peer(h.ys.at(k)))
        self.link.arrived(self.land1, self.s_core, h.other)
        for k in (2, 1, 3):
            i = h.ys.at(k)
            self.stage1[i] = (self.own1[i] + self.land1[i].astype(F32)).astype(BF16)
            self.link.start(self.stage1.at[i], self.land2.at[h.y], self.s_y, h.ys.peer(i))
        self.own2[...] = self.own1[h.y] + self.land1[h.y].astype(F32)
        self.link.sends(self.counts.at[pl.ds(FROM_Y, NY - 1)], self.c_y, h.other)
        self.link.sends(self.stage1.at[pl.ds(0, NY - 1)], self.s_y, h.other)

    def to_z(self):
        h = self.here
        counts = self.counts[CHIP]
        self.link.arrived(self.counts.at[pl.ds(FROM_Y, NY - 1)], self.c_y, h.other)
        for k in range(1, NY):
            counts = counts + self.counts[FROM_Y + h.ys.back(k)]
        self.counts[RING] = counts
        for owner in self.owners:

            @pl.when(h.z != owner)
            def _():
                self.link.start(self.counts.at[RING], self.counts.at[FROM_Z + h.z], self.c_z, h.zs.peer(owner))

        self.link.arrived(self.land2.at[pl.ds(0, NY - 1)], self.s_y, h.other)
        for j, owner in enumerate(self.owners):
            r, columns = j // SIDES, slice(j % SIDES * SIDE, (j % SIDES + 1) * SIDE)
            total = self.own2[r, :, columns]
            for k in range(1, NY):
                total = total + self.land2[h.ys.back(k), r, :, columns].astype(F32)
            self.stage2[j] = total.astype(BF16)

            @pl.when(h.z == owner)
            def _():
                self.own3[...] = total

            @pl.when(h.z != owner)
            def _():
                self.link.start(self.stage2.at[j], self.land3.at[h.z], self.s_z, h.zs.peer(owner))

        for count, when in ((PIECES - 1, self.owns), (PIECES, jnp.logical_not(self.owns))):
            self.link.sends(self.counts.at[pl.ds(FROM_Z, count)], self.c_z, h.other, when)
            self.link.sends(self.stage2.at[pl.ds(0, count)], self.s_z, h.other, when)

    def piece(self, index):
        side = pl.multiple_of(lax.rem(index, SIDES) * SIDE, LANES)
        return self.table.at[self.here.c, self.here.y, index // SIDES, :, pl.ds(side, SIDE)]

    def update(self):
        h = self.here
        self.link.sends(self.land3.at[pl.ds(0, NZ - 1)], self.g_z, h.other, self.owns)

        @pl.when(self.owns)
        def _():
            tally, total = self.counts[RING], self.own3[...]
            self.link.arrived(self.counts.at[pl.ds(FROM_Z, NZ - 1)], self.c_z, h.other)
            self.link.arrived(self.land3.at[pl.ds(0, NZ - 1)], self.s_z, h.other)
            for k in range(1, NZ):
                j = h.zs.back(k)
                tally = tally + self.counts[FROM_Z + j]
                total = total + self.land3[j].astype(F32)
            tile = self.index // SIDES
            lane = h.y * 32 + tile * 16
            found = iota((16, LANES), 1) == lane + iota((16, LANES), 0)
            counts = jnp.sum(jnp.where(found, tally, 0.0), axis=1, keepdims=True)
            fresh = 0.5 * self.change[...] + 0.5 * (total / (counts + 1.0))
            self.change[...] = fresh
            mine = self.piece(self.index)
            mine[...] = fresh.astype(BF16)
            for k in (4, 3, 5, 2, 6, 1, 7):
                self.link.start(mine, mine, self.g_z, h.zs.peer(h.zs.at(k)), self.g_z + tile)

    def gather_y(self):
        h = self.here
        for r in range(TILES):
            mine = self.table.at[h.c, h.y, r]
            own = jnp.logical_and(self.owns, self.index // SIDES == r)

            @pl.when(own)
            def _():
                self.link.arrived(mine.at[:, pl.ds(0, D - SIDE)], self.g_z + r, h.other)

            @pl.when(jnp.logical_not(own))
            def _():
                self.link.arrived(mine, self.g_z + r, h.other)

            for k in (2, 1, 3):
                self.link.start(mine, mine, self.g_y, h.ys.peer(h.ys.at(k)), self.g_y + k)
        mine = self.table.at[h.c, h.y]
        self.link.start(mine, mine, self.g_core, h.other)
        self.link.sends(self.table.at[h.c, pl.ds(0, NY - 1)], self.g_y, h.other)

    def gather_core(self):
        h = self.here
        for k in (1, 3, 2):
            here = self.table.at[h.c, h.ys.back(k)]
            self.link.arrived(here, self.g_y + k, h.other)
            self.link.start(here, here, self.g_core, h.other)
        self.link.sends(self.table.at[h.c], self.g_core, h.other)

    def gathered(self):
        self.link.arrived(self.table.at[1 - self.here.c], self.g_core, self.here.other)


class Route:
    def __init__(self, here, link, src, near, middle, got, mix=None):
        self.here, self.link = here, link
        self.src, self.near, self.middle, self.got, self.mix = src, near, middle, got, mix
        self.s_core, self.s_y, self.s_z = link.slots(1), link.slots(1), link.slots(1)

    def to_core(self):
        h = self.here
        self.link.start(self.src.at[1 - h.c], self.near, self.s_core, h.other)
        self.link.sends(self.near, self.s_core, h.other)

    def to_y(self):
        h = self.here
        self.link.arrived(self.near, self.s_core, h.other)
        for s, ref in enumerate((self.src.at[h.c], self.near)):
            for k in (2, 1, 3):
                i = h.ys.at(k)
                self.link.start(ref.at[i], self.middle.at[h.y, s], self.s_y, h.ys.peer(i))
            self.middle[h.y, s] = ref[h.y]
        self.link.sends(self.middle.at[pl.ds(0, NY - 1)], self.s_y, h.other)

    def to_z(self):
        h = self.here
        self.link.arrived(self.middle.at[pl.ds(0, NY - 1)], self.s_y, h.other)
        if self.mix is None:
            blocks = lambda j: self.middle.at[:, :, j]
        else:
            d, s = iota((SENDS, SENDS), 0), iota((SENDS, SENDS), 1)
            order = (s == ((d & 31) >> 2) * 32 + (d >> 5) * 4 + (d & 3)).astype(BF16)
            mixed = dot(order, self.middle[...].reshape(SENDS, WIDE)).astype(BF16)
            self.mix[...] = mixed.reshape(self.mix.shape)
            blocks = lambda j: self.mix.at[j]
        for k in (4, 3, 5, 2, 6, 1, 7):
            j = h.zs.at(k)
            self.link.start(blocks(j), self.got.at[h.z], self.s_z, h.zs.peer(j))
        self.got[h.z] = blocks(h.z)[...]
        self.link.sends(self.got.at[pl.ds(0, NZ - 1)], self.s_z, h.other)

    def finish(self):
        self.link.arrived(self.got.at[pl.ds(0, NZ - 1)], self.s_z, self.here.other)


def whole_kernel(
    corpus_any, c0_any, cand_ref, leaf_ref, slots_ref,
    table_any, out_ref,
    part, own1, land1, stage1, land2, own2, stage2, land3, own3, counts, change, table1, table2,
    corpus_ref, c0_ref, norm_ref, comp_ref, pick_ref, mixed_ref,
    wsend, wnear, wmiddle, wgot, rsend, rnear, rmiddle, rmix, rgot,
    share_ref, sums_ref, lands_ref, send, recv, fetch,
):
    h = Here()
    fetches = [pltpu.make_async_copy(corpus_any, corpus_ref, fetch.at[CHUNKS])]
    fetches += [pltpu.make_async_copy(c0_any.at[t], c0_ref.at[t], fetch.at[t]) for t in range(CHUNKS)]
    for copy in fetches[:2]:
        copy.start()
    greeted = h.greet()
    links = [Link(send, recv) for _ in range(CHUNKS + 1)]
    link = links[CHUNKS]
    bases = [link.slots(7 + TILES + NY) for _ in range(CHUNKS)]
    chunks = []
    for n in range(2 * CHUNKS):
        t = n % CHUNKS
        table = (table1 if n < CHUNKS else table2).at[t]
        refs = [r.at[n] for r in (part, own1, land1, stage1, land2, own2, stage2, land3, own3, counts)]
        chunks.append(Chunk(h, links[t], bases[t], t, *refs, change.at[t], table))
    weights_route = Route(h, link, wsend, wnear, wmiddle, wgot)
    corpus_route = Route(h, link, rsend, rnear, rmiddle, rgot, rmix)
    s_x = link.slots(1)
    cand = in_lanes(cand_ref) - h.x * (CENTS // BLOCK)
    change[...] = jnp.zeros_like(change)
    comp_ref[...] = jnp.zeros_like(comp_ref)
    fetches[0].wait()
    for copy in fetches[2:]:
        copy.start()
    norm_ref[...] = row_norms(corpus_ref[...])
    meta, stores = [], []

    def compute(n):
        t = n % CHUNKS
        if n < CHUNKS:
            fetches[1 + t].wait()
        cents = c0_ref[t]
        if n >= CHUNKS:
            cents = 0.5 * cents + table1[t].reshape(TILE, D).astype(F32)
        corpus = corpus_ref[...]
        weights, compact = tile_weights(cents, corpus, norm_ref[...], cand, t * (TILE // BLOCK))
        if n >= CHUNKS:
            comp_ref[...] += compact
        tally = dot(jnp.ones((8, ROWS), BF16), weights, 1, 1)
        left, right = tally[:1, :LANES], tally[:1, LANES:]
        chunks[n].counts[OWN] = jnp.where(h.c == 0, left, right)
        chunks[n].counts[AWAY] = jnp.where(h.c == 0, right, left)
        sums = dot(weights, corpus).reshape(NC, NY, TILES, 16, D)
        for s in range(NC):

            @pl.when(h.c == s)
            def _():
                chunks[n].own1[...] = sums[s]

            @pl.when(h.c != s)
            def _():
                chunks[n].part[...] = sums[s].astype(BF16)

        if n >= CHUNKS:
            links[t].finish()
        if n == 0:
            greeted()
        chunks[n].to_core()

    def prepare():
        owner, slot, rank = positions(in_lanes(leaf_ref), slots_ref[...])
        spot = ((owner & 1) * NY + ((owner >> 1) & 3)) * NZ + (owner >> 3)
        quarter = iota((1, ROWS), 1) >> 8
        fill = iota((BLOCK, ROWS), 0)
        meta.append(jnp.where(fill == 0, slot, jnp.where(fill == 1, cand.astype(F32), 0.0)))
        short = jnp.where(quarter == h.x, spot * 4 + rank, -1)
        whole = (iota((SENDS, ROWS), 0) == short).astype(BF16)
        folded = whole[:, :SENDS] + whole[:, SENDS : 2 * SENDS] + whole[:, 2 * SENDS : 3 * SENDS] + whole[:, 3 * SENDS :]
        mine = corpus_ref[pl.ds(pl.multiple_of(h.x * SENDS, SENDS), SENDS), :]
        marks = dot(whole, jnp.concatenate([jnp.zeros((BLOCK, ROWS), F32), meta[0]], axis=0).astype(BF16), 1, 1)
        rows = jnp.concatenate([dot(folded, mine), marks], axis=1).astype(BF16)
        rsend[...] = rows.reshape(rsend.shape)
        target = spot * 16 + quarter * 4 + rank
        for t in range(ROWS // TILE):
            pick_ref[t * TILE : (t + 1) * TILE, :] = (iota((TILE, ROWS), 0) + t * TILE == target).astype(BF16)
        corpus_route.to_core()

    def send_weights():
        load = jnp.concatenate([comp_ref[...], meta[0]], axis=0).astype(BF16)
        for s in range(NC):
            half = dot(pick_ref[s * ROWS // 2 : (s + 1) * ROWS // 2, :], load, 1, 1).astype(BF16)
            wsend[s] = half.reshape(wsend.shape[1:])
        weights_route.to_core()

    def receive_corpus():
        eye = (iota((LANES, LANES), 0) == iota((LANES, LANES), 1)).astype(BF16)
        corpus_route.finish()
        came = rgot[...].reshape(SENDS, WIDE)
        turned = dot(eye, came[:, D:], 1, 1)
        chosen = (iota((LEAF_DEV, SENDS), 0) == turned[BLOCK : BLOCK + 1].astype(jnp.int32)).astype(BF16)
        sums_ref[...] = dot(chosen, came[:, :D]).reshape(sums_ref.shape)

    def receive_weights():
        eye = (iota((LANES, LANES), 0) == iota((LANES, LANES), 1)).astype(BF16)
        weights_route.finish()
        turned = dot(eye, wgot[...].reshape(ROWS, LANES), 1, 1)
        weights, slot, block = turned[:BLOCK], turned[BLOCK : BLOCK + 1], turned[BLOCK + 1 : BLOCK + 2]
        chosen = jnp.where(iota((LEAF_DEV, ROWS), 0) == slot.astype(jnp.int32), 1.0, 0.0)
        tally = jnp.broadcast_to(jnp.sum(chosen, axis=1, keepdims=True), (LEAF_DEV, LANES))
        share_ref[...] = tally.reshape(share_ref.shape)
        chosen = chosen.astype(BF16)
        for b in range(0, CENTS // BLOCK, 2):
            both = jnp.concatenate([jnp.where(block == b + s, weights, 0.0) for s in range(2)], axis=0)
            mixed_ref[b // 2] = dot(chosen, both.astype(BF16), 1, 1)

    def leaves(t):
        stores.append(pltpu.make_async_copy(table2.at[t], table_any.at[t], fetch.at[t]))
        stores[-1].start()
        cents = 0.25 * c0_ref[t] + table2[t].reshape(TILE, D).astype(F32)
        half = cents.astype(BF16)
        mixed = jnp.concatenate([mixed_ref[2 * t], mixed_ref[2 * t + 1]], axis=1)
        high = mixed.astype(BF16)
        low = (mixed - high.astype(F32)).astype(BF16)
        sums_ref[...] -= (dot(high, half) + dot(low, half)).reshape(sums_ref.shape)

    steps = dict(
        K=compute,
        Y=lambda n: chunks[n].to_y(),
        Z=lambda n: chunks[n].to_z(),
        U=lambda n: chunks[n].update(),
        G=lambda n: chunks[n].gather_y(),
        H=lambda n: chunks[n].gather_core(),
        W=lambda n: chunks[n].gathered(),
        L=lambda n: leaves(n - CHUNKS),
        c=lambda n: corpus_route.to_y() if n == 1 else corpus_route.to_z(),
        w=lambda n: weights_route.to_y() if n == 1 else weights_route.to_z(),
        P=lambda n: prepare(),
        Q=lambda n: send_weights(),
        R=lambda n: receive_weights(),
        S=lambda n: receive_corpus(),
    )
    for step in " ".join(ORDER).split():
        steps[step[0]](int(step[1:] or 0))
    for k in (2, 1, 3):
        i = h.xs.at(k)
        link.start(sums_ref.at[i], lands_ref.at[h.x], s_x, h.xs.peer(i))
    link.sends(lands_ref.at[pl.ds(0, NX - 1)], s_x, h.other)
    total = sums_ref[h.x]
    for each in links:
        each.finish()
    for copy in stores:
        copy.wait()
    link.arrived(lands_ref.at[pl.ds(0, NX - 1)], s_x, h.other)
    for k in range(1, NX):
        total = total + lands_ref[h.xs.back(k)]
    out_ref[...] = total / (share_ref[h.x][:, :1] + 1.0)


def on_device(corpus, initial_centroids, cand_block, leaf_ids, slot_table):
    per = LEAF_DEV // NX
    steps = 2 * CHUNKS
    block = (NY, TILES, 16, D)
    scratch = [
        pltpu.VMEM((steps, *block), BF16),
        pltpu.VMEM((steps, *block), F32),
        pltpu.VMEM((steps, *block), BF16),
        pltpu.VMEM((steps, *block), BF16),
        pltpu.VMEM((steps, *block), BF16),
        pltpu.VMEM((steps, *block[1:]), F32),
        pltpu.VMEM((steps, PIECES, 16, SIDE), BF16),
        pltpu.VMEM((steps, NZ, 16, SIDE), BF16),
        pltpu.VMEM((steps, 16, SIDE), F32),
        pltpu.VMEM((steps, FROM_Z + NZ, 1, LANES), F32),
        pltpu.VMEM((CHUNKS, 16, SIDE), F32),
        pltpu.VMEM((CHUNKS, NC, *block), BF16),
        pltpu.VMEM((CHUNKS, NC, *block), BF16),
        pltpu.VMEM((ROWS, D), BF16),
        pltpu.VMEM((CHUNKS, TILE, D), F32),
        pltpu.VMEM((1, ROWS), F32),
        pltpu.VMEM((BLOCK, ROWS), F32),
        pltpu.VMEM((ROWS, ROWS), BF16),
        pltpu.VMEM((CENTS // LANES, LEAF_DEV, LANES), F32),
        pltpu.VMEM((NC, NY, NZ, 16, LANES), BF16),
        pltpu.VMEM((NY, NZ, 16, LANES), BF16),
        pltpu.VMEM((NY, NC, NZ, 16, LANES), BF16),
        pltpu.VMEM((NZ, NY, NC, 16, LANES), BF16),
        pltpu.VMEM((NC, NY, 32, WIDE), BF16),
        pltpu.VMEM((NY, 32, WIDE), BF16),
        pltpu.VMEM((NY, NC, 32, WIDE), BF16),
        pltpu.VMEM((NZ, 32, WIDE), BF16),
        pltpu.VMEM((NZ, 32, WIDE), BF16),
        pltpu.VMEM((NX, per, LANES), F32),
        pltpu.VMEM((NX, per, D), F32),
        pltpu.VMEM((NX, per, D), F32),
        pltpu.SemaphoreType.DMA((SEMAPHORES,)),
        pltpu.SemaphoreType.DMA((SEMAPHORES,)),
        pltpu.SemaphoreType.DMA((CHUNKS + 1,)),
    ]
    away = pl.BlockSpec(memory_space=pl.ANY)
    centroids, leaves = pl.pallas_call(
        whole_kernel,
        out_shape=[
            jax.ShapeDtypeStruct((CHUNKS, NC, *block), BF16),
            jax.ShapeDtypeStruct((per, D), F32),
        ],
        in_specs=[away] * 2 + [ANYWHERE] * 3,
        out_specs=[away, ANYWHERE],
        scratch_shapes=scratch,
        compiler_params=pltpu.CompilerParams(collective_id=1, has_side_effects=True, vmem_limit_bytes=LIMIT),
        name="whole",
    )(
        corpus,
        initial_centroids.reshape(CHUNKS, TILE, D),
        cand_block.reshape(-1, LANES),
        leaf_ids.reshape(-1, LANES),
        slot_table.reshape(-1, LANES),
    )
    return 0.25 * initial_centroids + centroids.reshape(CENTS, D).astype(F32), leaves


def solution(mesh):
    in_specs = (P("rows", None), P("rep", None), P("rows"), P("rows"), P())
    out_specs = (P("rep", None), P(("rows", "rep"), None))
    return jax.shard_map(
        on_device, mesh=mesh, in_specs=in_specs, out_specs=out_specs, check_vma=False
    )
```

```python
import functools

import jax
import jax.numpy as jnp
from jax import lax
from jax.experimental import pallas as pl
from jax.experimental.pallas import tpu as pltpu
from jax.sharding import PartitionSpec as P

D = 768
BLOCK = 64
LANES = 128
WIDE = D + LANES
NZ, NY, NC, NX = 8, 4, 2, 4
OWNERS = NZ * NY * NC
ROWS = 1024
CENTS = 1024
SENDS = 256
TILE = 256
LEAF_DEV = 64
CHUNKS, TILES = 4, 2
SIDES = 3
SIDE = D // SIDES
PIECES = TILES * SIDES
OWN, AWAY, NEAR, CHIP, RING, FROM_Y = range(6)
FROM_Z = FROM_Y + NY
F32, BF16 = jnp.float32, jnp.bfloat16
MESH = pl.DeviceIdType.MESH
ANYWHERE = pl.BlockSpec(memory_space=pltpu.VMEM)
LIMIT = 56 * 1024 * 1024
SEMAPHORES = CHUNKS * (6 + TILES + NY + 1) + 2 * 3 + 1
ORDER = (
    "K0 K1 Y0 K2", "Y1 K3 Y2 Y3", "Z0 P Z1 Z2", "U0 Z3 c1 U1", "U2 G0 U3 G1", "c2 G2 H0 W0",
    "K4 G3 H1 Y4", "W1 K5 H2 Y5", "W2 K6 H3 Y6", "Z4 W3 K7 Y7", "Z5 Q Z6 U4", "Z7 w1 U5 G4",
    "U6 U7 w2 G5", "G6 H4 G7 S", "H5 H6 W4 W5", "H7 R L4 L5", "W6 L6 W7 L7",
)


def iota(shape, axis):
    return lax.broadcasted_iota(jnp.int32, shape, axis)


def dot(a, b, ca=1, cb=0):
    return lax.dot_general(a, b, (((ca,), (cb,)), ((), ())), preferred_element_type=F32)


def place():
    r = lax.axis_index("rows")
    return r // (NY * NC), lax.rem(r // NC, NY), lax.rem(r, NC), lax.axis_index("rep")


def row_index(z, y, c):
    return (z * NY + y) * NC + c


def row_norms(corpus):
    square = jnp.square(corpus.astype(F32))
    high = square.astype(BF16)
    low = (square - high.astype(F32)).astype(BF16)
    ones = jnp.ones((8, D), BF16)
    return (dot(ones, high, 1, 1) + dot(ones, low, 1, 1))[:1]


def tile_weights(cents, corpus, norms, cand, first_block):
    centre = jnp.sum(cents * cents, axis=1, keepdims=True) * (1.0 / D)
    products = dot(cents.astype(BF16), corpus, 1, 1)
    kernel = 1.0 / ((norms + centre) - products * (2.0 / D))
    parts, compact = [], None
    for b in range(TILE // BLOCK):
        piece = kernel[b * BLOCK : (b + 1) * BLOCK]
        total = jnp.sum(piece, axis=0, keepdims=True)
        piece = (piece * jnp.where(cand == first_block + b, 1.0 / total, 0.0)).astype(BF16)
        parts.append(piece)
        wide = piece.astype(F32)
        compact = wide if compact is None else compact + wide
    return jnp.concatenate(parts, axis=0), compact


def in_lanes(ref):
    values = ref[...]
    return jnp.concatenate([values[i : i + 1] for i in range(values.shape[0])], axis=1)


def positions(leaf, slots):
    upper = (iota((slots.shape[0], ROWS), 0) == (leaf >> 7)).astype(BF16)
    lower = iota((slots.shape[1], ROWS), 0) == (leaf & 127)

    def look(values):
        found = dot(values.astype(F32).astype(BF16), upper, 0, 0)
        return jnp.sum(jnp.where(lower, found, 0.0), axis=0, keepdims=True)

    owner, slot = look(slots >> 6).astype(jnp.int32), look(slots & 63)
    hits = iota((OWNERS, ROWS), 0) == owner
    before = (iota((SENDS, SENDS), 0) < iota((SENDS, SENDS), 1)).astype(BF16)
    ranks = []
    for q in range(ROWS // SENDS):
        own = hits[:, q * SENDS : (q + 1) * SENDS]
        ahead = dot(jnp.where(own, 1.0, 0.0).astype(BF16), before)
        ranks.append(jnp.sum(jnp.where(own, ahead, 0.0), axis=0, keepdims=True))
    return owner, slot, jnp.concatenate(ranks, axis=1).astype(jnp.int32)


class Link:
    def __init__(self, send, recv):
        self.send, self.recv, self.used, self.sent = send, recv, 0, []

    def slots(self, count):
        first = self.used
        self.used += count
        return first

    def make(self, src, dst, out, into, device):
        return pltpu.make_async_remote_copy(
            src_ref=src, dst_ref=dst, send_sem=self.send.at[out], recv_sem=self.recv.at[into],
            device_id=device, device_id_type=MESH,
        )

    def start(self, src, dst, slot, device, into=None):
        self.make(src, dst, slot, slot if into is None else into, device).start()

    def arrived(self, whole, slot, device):
        self.make(whole, whole, slot, slot, device).wait_recv()

    def sends(self, whole, slot, device, when=None):
        self.sent.append((self.make(whole, whole, slot, slot, device), when))

    def finish(self):
        for copy, when in self.sent:
            if when is None:
                copy.wait_send()
            else:
                pl.when(when)(copy.wait_send)
        self.sent.clear()


class Axis:
    def __init__(self, size, me, peer):
        self.size, self.me, self.peer = size, me, peer

    def at(self, k):
        return lax.rem(self.me + k, self.size)

    def back(self, k):
        return lax.rem(self.me + self.size - k, self.size)


class Here:
    def __init__(self):
        z, y, c, x = place()
        self.z, self.y, self.c, self.x = z, y, c, x
        row = row_index(z, y, c)
        self.zs = Axis(NZ, z, lambda i: (row_index(i, y, c), x))
        self.ys = Axis(NY, y, lambda i: (row_index(z, i, c), x))
        self.xs = Axis(NX, x, lambda i: (row, i))
        self.other = (row_index(z, y, 1 - c), x)

    def greet(self):
        barrier = pltpu.get_barrier_semaphore()
        peers = [self.other] + [a.peer(a.at(k)) for a in (self.zs, self.ys, self.xs) for k in range(1, a.size)]
        for peer in peers:
            pl.semaphore_signal(barrier, inc=1, device_id=peer, device_id_type=MESH)
        return lambda: pl.semaphore_wait(barrier, len(peers))


class Chunk:
    def __init__(self, here, link, base, t, part, own1, land1, stage1, land2, own2, stage2, land3, own3, counts, change, table):
        self.here, self.link, self.t = here, link, t
        self.part, self.own1, self.land1, self.stage1, self.land2, self.own2 = part, own1, land1, stage1, land2, own2
        self.stage2, self.land3, self.own3, self.counts, self.change, self.table = stage2, land3, own3, counts, change, table
        self.c_core, self.c_y, self.c_z, self.s_core, self.s_y, self.s_z = range(base, base + 6)
        self.g_z, self.g_y, self.g_core = base + 6, base + 6 + TILES, base + 6 + TILES + NY
        self.owners = [(j + 2 * t) % NZ for j in range(PIECES)]
        self.index = lax.rem(here.z + (NZ - 2 * t), NZ)
        self.owns = self.index < PIECES

    def to_core(self):
        h = self.here
        self.link.start(self.counts.at[AWAY], self.counts.at[NEAR], self.c_core, h.other)
        self.link.start(self.part, self.land1, self.s_core, h.other)
        self.link.sends(self.counts.at[AWAY], self.c_core, h.other)
        self.link.sends(self.part, self.s_core, h.other)

    def to_y(self):
        h = self.here
        self.link.arrived(self.counts.at[NEAR], self.c_core, h.other)
        self.counts[CHIP] = self.counts[OWN] + self.counts[NEAR]
        for k in (2, 1, 3):
            self.link.start(self.counts.at[CHIP], self.counts.at[FROM_Y + h.y], self.c_y, h.ys.peer(h.ys.at(k)))
        self.link.arrived(self.land1, self.s_core, h.other)
        for k in (2, 1, 3):
            i = h.ys.at(k)
            self.stage1[i] = (self.own1[i] + self.land1[i].astype(F32)).astype(BF16)
            self.link.start(self.stage1.at[i], self.land2.at[h.y], self.s_y, h.ys.peer(i))
        self.own2[...] = self.own1[h.y] + self.land1[h.y].astype(F32)
        self.link.sends(self.counts.at[pl.ds(FROM_Y, NY - 1)], self.c_y, h.other)
        self.link.sends(self.stage1.at[pl.ds(0, NY - 1)], self.s_y, h.other)

    def to_z(self):
        h = self.here
        counts = self.counts[CHIP]
        self.link.arrived(self.counts.at[pl.ds(FROM_Y, NY - 1)], self.c_y, h.other)
        for k in range(1, NY):
            counts = counts + self.counts[FROM_Y + h.ys.back(k)]
        self.counts[RING] = counts
        for owner in self.owners:

            @pl.when(h.z != owner)
            def _():
                self.link.start(self.counts.at[RING], self.counts.at[FROM_Z + h.z], self.c_z, h.zs.peer(owner))

        self.link.arrived(self.land2.at[pl.ds(0, NY - 1)], self.s_y, h.other)
        for j, owner in enumerate(self.owners):
            r, columns = j // SIDES, slice(j % SIDES * SIDE, (j % SIDES + 1) * SIDE)
            total = self.own2[r, :, columns]
            for k in range(1, NY):
                total = total + self.land2[h.ys.back(k), r, :, columns].astype(F32)
            self.stage2[j] = total.astype(BF16)

            @pl.when(h.z == owner)
            def _():
                self.own3[...] = total

            @pl.when(h.z != owner)
            def _():
                self.link.start(self.stage2.at[j], self.land3.at[h.z], self.s_z, h.zs.peer(owner))

        for count, when in ((PIECES - 1, self.owns), (PIECES, jnp.logical_not(self.owns))):
            self.link.sends(self.counts.at[pl.ds(FROM_Z, count)], self.c_z, h.other, when)
            self.link.sends(self.stage2.at[pl.ds(0, count)], self.s_z, h.other, when)

    def piece(self, index):
        side = pl.multiple_of(lax.rem(index, SIDES) * SIDE, LANES)
        return self.table.at[self.here.c, self.here.y, index // SIDES, :, pl.ds(side, SIDE)]

    def update(self):
        h = self.here
        self.link.sends(self.land3.at[pl.ds(0, NZ - 1)], self.g_z, h.other, self.owns)

        @pl.when(self.owns)
        def _():
            tally, total = self.counts[RING], self.own3[...]
            self.link.arrived(self.counts.at[pl.ds(FROM_Z, NZ - 1)], self.c_z, h.other)
            self.link.arrived(self.land3.at[pl.ds(0, NZ - 1)], self.s_z, h.other)
            for k in range(1, NZ):
                j = h.zs.back(k)
                tally = tally + self.counts[FROM_Z + j]
                total = total + self.land3[j].astype(F32)
            tile = self.index // SIDES
            lane = h.y * 32 + tile * 16
            found = iota((16, LANES), 1) == lane + iota((16, LANES), 0)
            counts = jnp.sum(jnp.where(found, tally, 0.0), axis=1, keepdims=True)
            fresh = 0.5 * self.change[...] + 0.5 * (total / (counts + 1.0))
            self.change[...] = fresh
            mine = self.piece(self.index)
            mine[...] = fresh.astype(BF16)
            for k in (4, 3, 5, 2, 6, 1, 7):
                self.link.start(mine, mine, self.g_z, h.zs.peer(h.zs.at(k)), self.g_z + tile)

    def gather_y(self):
        h = self.here
        for r in range(TILES):
            mine = self.table.at[h.c, h.y, r]
            own = jnp.logical_and(self.owns, self.index // SIDES == r)

            @pl.when(own)
            def _():
                self.link.arrived(mine.at[:, pl.ds(0, D - SIDE)], self.g_z + r, h.other)

            @pl.when(jnp.logical_not(own))
            def _():
                self.link.arrived(mine, self.g_z + r, h.other)

            for k in (2, 1, 3):
                self.link.start(mine, mine, self.g_y, h.ys.peer(h.ys.at(k)), self.g_y + k)
        mine = self.table.at[h.c, h.y]
        self.link.start(mine, mine, self.g_core, h.other)
        self.link.sends(self.table.at[h.c, pl.ds(0, NY - 1)], self.g_y, h.other)

    def gather_core(self):
        h = self.here
        for k in (1, 3, 2):
            here = self.table.at[h.c, h.ys.back(k)]
            self.link.arrived(here, self.g_y + k, h.other)
            self.link.start(here, here, self.g_core, h.other)
        self.link.sends(self.table.at[h.c], self.g_core, h.other)

    def gathered(self):
        self.link.arrived(self.table.at[1 - self.here.c], self.g_core, self.here.other)


class Route:
    def __init__(self, here, link, src, near, middle, got, mix=None):
        self.here, self.link = here, link
        self.src, self.near, self.middle, self.got, self.mix = src, near, middle, got, mix
        self.s_core, self.s_y, self.s_z = link.slots(1), link.slots(1), link.slots(1)

    def to_core(self):
        h = self.here
        self.link.start(self.src.at[1 - h.c], self.near, self.s_core, h.other)
        self.link.sends(self.near, self.s_core, h.other)

    def to_y(self):
        h = self.here
        self.link.arrived(self.near, self.s_core, h.other)
        for s, ref in enumerate((self.src.at[h.c], self.near)):
            for k in (2, 1, 3):
                i = h.ys.at(k)
                self.link.start(ref.at[i], self.middle.at[h.y, s], self.s_y, h.ys.peer(i))
            self.middle[h.y, s] = ref[h.y]
        self.link.sends(self.middle.at[pl.ds(0, NY - 1)], self.s_y, h.other)

    def to_z(self):
        h = self.here
        self.link.arrived(self.middle.at[pl.ds(0, NY - 1)], self.s_y, h.other)
        if self.mix is None:
            blocks = lambda j: self.middle.at[:, :, j]
        else:
            d, s = iota((SENDS, SENDS), 0), iota((SENDS, SENDS), 1)
            order = (s == ((d & 31) >> 2) * 32 + (d >> 5) * 4 + (d & 3)).astype(BF16)
            mixed = dot(order, self.middle[...].reshape(SENDS, WIDE)).astype(BF16)
            self.mix[...] = mixed.reshape(self.mix.shape)
            blocks = lambda j: self.mix.at[j]
        for k in (4, 3, 5, 2, 6, 1, 7):
            j = h.zs.at(k)
            self.link.start(blocks(j), self.got.at[h.z], self.s_z, h.zs.peer(j))
        self.got[h.z] = blocks(h.z)[...]
        self.link.sends(self.got.at[pl.ds(0, NZ - 1)], self.s_z, h.other)

    def finish(self):
        self.link.arrived(self.got.at[pl.ds(0, NZ - 1)], self.s_z, self.here.other)


def whole_kernel(
    corpus_any, c0_any, cand_ref, leaf_ref, slots_ref,
    table_any, out_ref,
    part, own1, land1, stage1, land2, own2, stage2, land3, own3, counts, change, table1, table2,
    corpus_ref, c0_ref, norm_ref, comp_ref, pick_ref, mixed_ref,
    wsend, wnear, wmiddle, wgot, rsend, rnear, rmiddle, rmix, rgot,
    share_ref, sums_ref, lands_ref, send, recv, fetch,
):
    h = Here()
    fetches = [pltpu.make_async_copy(corpus_any, corpus_ref, fetch.at[CHUNKS])]
    fetches += [pltpu.make_async_copy(c0_any.at[t], c0_ref.at[t], fetch.at[t]) for t in range(CHUNKS)]
    for copy in fetches[:2]:
        copy.start()
    greeted = h.greet()
    links = [Link(send, recv) for _ in range(CHUNKS + 1)]
    link = links[CHUNKS]
    bases = [link.slots(7 + TILES + NY) for _ in range(CHUNKS)]
    chunks = []
    for n in range(2 * CHUNKS):
        t = n % CHUNKS
        table = (table1 if n < CHUNKS else table2).at[t]
        refs = [r.at[n] for r in (part, own1, land1, stage1, land2, own2, stage2, land3, own3, counts)]
        chunks.append(Chunk(h, links[t], bases[t], t, *refs, change.at[t], table))
    weights_route = Route(h, link, wsend, wnear, wmiddle, wgot)
    corpus_route = Route(h, link, rsend, rnear, rmiddle, rgot, rmix)
    s_x = link.slots(1)
    cand = in_lanes(cand_ref) - h.x * (CENTS // BLOCK)
    change[...] = jnp.zeros_like(change)
    comp_ref[...] = jnp.zeros_like(comp_ref)
    fetches[0].wait()
    for copy in fetches[2:]:
        copy.start()
    norm_ref[...] = 1.0 + row_norms(corpus_ref[...]) * (1.0 / D)
    meta, stores = [], []

    def compute(n):
        t = n % CHUNKS
        if n < CHUNKS:
            fetches[1 + t].wait()
        cents = c0_ref[t]
        if n >= CHUNKS:
            cents = 0.5 * cents + table1[t].reshape(TILE, D).astype(F32)
        corpus = corpus_ref[...]
        weights, compact = tile_weights(cents, corpus, norm_ref[...], cand, t * (TILE // BLOCK))
        if n >= CHUNKS:
            comp_ref[...] += compact
        tally = dot(jnp.ones((8, ROWS), BF16), weights, 1, 1)
        left, right = tally[:1, :LANES], tally[:1, LANES:]
        chunks[n].counts[OWN] = jnp.where(h.c == 0, left, right)
        chunks[n].counts[AWAY] = jnp.where(h.c == 0, right, left)
        sums = dot(weights, corpus).reshape(NC, NY, TILES, 16, D)
        for s in range(NC):

            @pl.when(h.c == s)
            def _():
                chunks[n].own1[...] = sums[s]

            @pl.when(h.c != s)
            def _():
                chunks[n].part[...] = sums[s].astype(BF16)

        if n >= CHUNKS:
            links[t].finish()
        if n == 0:
            greeted()
        chunks[n].to_core()

    def prepare():
        owner, slot, rank = positions(in_lanes(leaf_ref), slots_ref[...])
        spot = ((owner & 1) * NY + ((owner >> 1) & 3)) * NZ + (owner >> 3)
        quarter = iota((1, ROWS), 1) >> 8
        fill = iota((BLOCK, ROWS), 0)
        meta.append(jnp.where(fill == 0, slot, jnp.where(fill == 1, cand.astype(F32), 0.0)))
        short = jnp.where(quarter == h.x, spot * 4 + rank, -1)
        whole = (iota((SENDS, ROWS), 0) == short).astype(BF16)
        folded = whole[:, :SENDS] + whole[:, SENDS : 2 * SENDS] + whole[:, 2 * SENDS : 3 * SENDS] + whole[:, 3 * SENDS :]
        mine = corpus_ref[pl.ds(pl.multiple_of(h.x * SENDS, SENDS), SENDS), :]
        marks = dot(whole, jnp.concatenate([jnp.zeros((BLOCK, ROWS), F32), meta[0]], axis=0).astype(BF16), 1, 1)
        rows = jnp.concatenate([dot(folded, mine), marks], axis=1).astype(BF16)
        rsend[...] = rows.reshape(rsend.shape)
        target = spot * 16 + quarter * 4 + rank
        for t in range(ROWS // TILE):
            pick_ref[t * TILE : (t + 1) * TILE, :] = (iota((TILE, ROWS), 0) + t * TILE == target).astype(BF16)
        corpus_route.to_core()

    def send_weights():
        load = jnp.concatenate([comp_ref[...], meta[0]], axis=0).astype(BF16)
        for s in range(NC):
            half = dot(pick_ref[s * ROWS // 2 : (s + 1) * ROWS // 2, :], load, 1, 1).astype(BF16)
            wsend[s] = half.reshape(wsend.shape[1:])
        weights_route.to_core()

    def receive_corpus():
        eye = (iota((LANES, LANES), 0) == iota((LANES, LANES), 1)).astype(BF16)
        corpus_route.finish()
        came = rgot[...].reshape(SENDS, WIDE)
        turned = dot(eye, came[:, D:], 1, 1)
        chosen = (iota((LEAF_DEV, SENDS), 0) == turned[BLOCK : BLOCK + 1].astype(jnp.int32)).astype(BF16)
        sums_ref[...] = dot(chosen, came[:, :D]).reshape(sums_ref.shape)

    def receive_weights():
        eye = (iota((LANES, LANES), 0) == iota((LANES, LANES), 1)).astype(BF16)
        weights_route.finish()
        turned = dot(eye, wgot[...].reshape(ROWS, LANES), 1, 1)
        weights, slot, block = turned[:BLOCK], turned[BLOCK : BLOCK + 1], turned[BLOCK + 1 : BLOCK + 2]
        chosen = jnp.where(iota((LEAF_DEV, ROWS), 0) == slot.astype(jnp.int32), 1.0, 0.0)
        tally = jnp.broadcast_to(jnp.sum(chosen, axis=1, keepdims=True), (LEAF_DEV, LANES))
        share_ref[...] = tally.reshape(share_ref.shape)
        chosen = chosen.astype(BF16)
        for b in range(0, CENTS // BLOCK, 2):
            both = jnp.concatenate([jnp.where(block == b + s, weights, 0.0) for s in range(2)], axis=0)
            mixed_ref[b // 2] = dot(chosen, both.astype(BF16), 1, 1)

    def leaves(t):
        stores.append(pltpu.make_async_copy(table2.at[t], table_any.at[t], fetch.at[t]))
        stores[-1].start()
        cents = 0.25 * c0_ref[t] + table2[t].reshape(TILE, D).astype(F32)
        half = cents.astype(BF16)
        mixed = jnp.concatenate([mixed_ref[2 * t], mixed_ref[2 * t + 1]], axis=1)
        high = mixed.astype(BF16)
        low = (mixed - high.astype(F32)).astype(BF16)
        sums_ref[...] -= (dot(high, half) + dot(low, half)).reshape(sums_ref.shape)

    steps = dict(
        K=compute,
        Y=lambda n: chunks[n].to_y(),
        Z=lambda n: chunks[n].to_z(),
        U=lambda n: chunks[n].update(),
        G=lambda n: chunks[n].gather_y(),
        H=lambda n: chunks[n].gather_core(),
        W=lambda n: chunks[n].gathered(),
        L=lambda n: leaves(n - CHUNKS),
        c=lambda n: corpus_route.to_y() if n == 1 else corpus_route.to_z(),
        w=lambda n: weights_route.to_y() if n == 1 else weights_route.to_z(),
        P=lambda n: prepare(),
        Q=lambda n: send_weights(),
        R=lambda n: receive_weights(),
        S=lambda n: receive_corpus(),
    )
    for step in " ".join(ORDER).split():
        steps[step[0]](int(step[1:] or 0))
    for k in (2, 1, 3):
        i = h.xs.at(k)
        link.start(sums_ref.at[i], lands_ref.at[h.x], s_x, h.xs.peer(i))
    link.sends(lands_ref.at[pl.ds(0, NX - 1)], s_x, h.other)
    total = sums_ref[h.x]
    for each in links:
        each.finish()
    for copy in stores:
        copy.wait()
    link.arrived(lands_ref.at[pl.ds(0, NX - 1)], s_x, h.other)
    for k in range(1, NX):
        total = total + lands_ref[h.xs.back(k)]
    out_ref[...] = total / (share_ref[h.x][:, :1] + 1.0)


def on_device(corpus, initial_centroids, cand_block, leaf_ids, slot_table):
    per = LEAF_DEV // NX
    steps = 2 * CHUNKS
    block = (NY, TILES, 16, D)
    scratch = [
        pltpu.VMEM((steps, *block), BF16),
        pltpu.VMEM((steps, *block), F32),
        pltpu.VMEM((steps, *block), BF16),
        pltpu.VMEM((steps, *block), BF16),
        pltpu.VMEM((steps, *block), BF16),
        pltpu.VMEM((steps, *block[1:]), F32),
        pltpu.VMEM((steps, PIECES, 16, SIDE), BF16),
        pltpu.VMEM((steps, NZ, 16, SIDE), BF16),
        pltpu.VMEM((steps, 16, SIDE), F32),
        pltpu.VMEM((steps, FROM_Z + NZ, 1, LANES), F32),
        pltpu.VMEM((CHUNKS, 16, SIDE), F32),
        pltpu.VMEM((CHUNKS, NC, *block), BF16),
        pltpu.VMEM((CHUNKS, NC, *block), BF16),
        pltpu.VMEM((ROWS, D), BF16),
        pltpu.VMEM((CHUNKS, TILE, D), F32),
        pltpu.VMEM((1, ROWS), F32),
        pltpu.VMEM((BLOCK, ROWS), F32),
        pltpu.VMEM((ROWS, ROWS), BF16),
        pltpu.VMEM((CENTS // LANES, LEAF_DEV, LANES), F32),
        pltpu.VMEM((NC, NY, NZ, 16, LANES), BF16),
        pltpu.VMEM((NY, NZ, 16, LANES), BF16),
        pltpu.VMEM((NY, NC, NZ, 16, LANES), BF16),
        pltpu.VMEM((NZ, NY, NC, 16, LANES), BF16),
        pltpu.VMEM((NC, NY, 32, WIDE), BF16),
        pltpu.VMEM((NY, 32, WIDE), BF16),
        pltpu.VMEM((NY, NC, 32, WIDE), BF16),
        pltpu.VMEM((NZ, 32, WIDE), BF16),
        pltpu.VMEM((NZ, 32, WIDE), BF16),
        pltpu.VMEM((NX, per, LANES), F32),
        pltpu.VMEM((NX, per, D), F32),
        pltpu.VMEM((NX, per, D), F32),
        pltpu.SemaphoreType.DMA((SEMAPHORES,)),
        pltpu.SemaphoreType.DMA((SEMAPHORES,)),
        pltpu.SemaphoreType.DMA((CHUNKS + 1,)),
    ]
    away = pl.BlockSpec(memory_space=pl.ANY)
    centroids, leaves = pl.pallas_call(
        whole_kernel,
        out_shape=[
            jax.ShapeDtypeStruct((CHUNKS, NC, *block), BF16),
            jax.ShapeDtypeStruct((per, D), F32),
        ],
        in_specs=[away] * 2 + [ANYWHERE] * 3,
        out_specs=[away, ANYWHERE],
        scratch_shapes=scratch,
        compiler_params=pltpu.CompilerParams(collective_id=1, has_side_effects=True, vmem_limit_bytes=LIMIT),
        name="whole",
    )(
        corpus,
        initial_centroids.reshape(CHUNKS, TILE, D),
        cand_block.reshape(-1, LANES),
        leaf_ids.reshape(-1, LANES),
        slot_table.reshape(-1, LANES),
    )
    return 0.25 * initial_centroids + centroids.reshape(CENTS, D).astype(F32), leaves


def solution(mesh):
    in_specs = (P("rows", None), P("rep", None), P("rows"), P("rows"), P())
    out_specs = (P("rep", None), P(("rows", "rep"), None))
    return jax.shard_map(
        on_device, mesh=mesh, in_specs=in_specs, out_specs=out_specs, check_vma=False
    )
```
